128 devices in a mesh: seq: 16 (over z_hi, x, core), chan: 8 (over z_lo, y).
Axes of the slice: x: 4, y: 4, z: 4 (z_hi: 2, z_lo: 2; z = z_hi * 2 + z_lo), core: 2. Of those that a mesh axis runs over, the one named last changes fastest.
Arguments:
- tokens: bfloat16 [4096, 8192], P('seq', 'chan'), may hold values from -6 to 6
- input_weight: bfloat16 [3, 8192, 8192], P(None, 'seq', 'chan'), may hold values from -0.0625 to 0.0625
- filter_taps: float32 [128, 8192], P(None, 'chan'), may hold values from -0.9 to 0.9
- decay_rates: float32 [8192], P('chan'), may hold values from 0.003 to 0.3
- skip_gain: float32 [8192], P('chan'), may hold values from 0.5 to 1.5
- owners: int32 [512, 1], P('seq'), may hold values from 0 to 15; in each aligned block of 32 rows (0 to 31, 32 to 63, ...) at most 2 rows name the same one
Outputs:
- gated: bfloat16 [4096, 8192], P('seq', 'chan')
- handed: bfloat16 [512, 8, 8192], P('seq', None, 'chan')
The draws below stay inside these ranges and needn't reach their ends.
Inputs may be any that keep to these rules, and one draw needn't show every extreme that they name: Among the 32 pages of one device each of the 16 owners is named exactly 2 times, so every row of handed is filled.
All inputs are finite; a program needn't handle non-finite values.
Results may differ from the reference program's by a relative error of at most 0.018.
Values may be sent and summed in bfloat16 or wider, within the bound.
A program may use at most 128 MiB of HBM per device.

```python
import math
import jax
import jax.numpy as jnp
import numpy as np
from jax import lax

D = 8192
FLT = 128
PAGE_ROWS = 8
CAP = 2
PAGES_DEV = 32
TOKENS = 4096
PAGES = 512
N_SEQ = 16


def level_of(rng, dims, cuts, least, top_value):
    factor_of, own = 1.0, jax.random.fold_in(rng, 6)
    for position, parts in cuts:
        steps = jnp.exp(jax.random.uniform(jax.random.fold_in(own, position), (parts,), jnp.float32, least / len(cuts), top_value / len(cuts)))
        factor_of = factor_of * jnp.repeat(steps, dims[position] // parts).reshape([-1 if axis == position else 1 for axis in range(len(dims))])
    return factor_of


def assign_block(own_key, own, number, rows, amount, top, bound, skew):
    ranking = jax.random.permutation(own_key, amount)
    crowded, usual = portions_of(amount, rows * top, bound, skew, True), portions_of(amount, rows * top, bound, skew, False)
    places = jnp.arange(amount)

    def named(lengths, offset_by):
        used = int((lengths > 0).sum())
        fixed = max(1, used // 4)
        moved = fixed + (places - fixed + offset_by * (used - fixed)) % max(1, amount - fixed)
        return jnp.zeros((amount,), jnp.int32).at[ranking[jnp.where(places < fixed, places, moved)]].set(jnp.asarray(lengths, jnp.int32))

    lengths = jnp.where(number % 4 == 0, named(crowded, number // 4), named(usual, number - number // 4 - 1))
    mixed = jax.random.permutation(jax.random.fold_in(own, 3), amount)
    giver, taker = mixed[0:amount // 2 * 2:2], mixed[1:amount // 2 * 2:2]
    margin = jnp.minimum(lengths[giver] - 1, bound - lengths[taker]) // 2
    margin = jnp.where((giver == ranking[0]) | (taker == ranking[0]) | (lengths[taker] == 0), 0, jnp.maximum(margin, 0))
    moved = jax.random.randint(jax.random.fold_in(own, 4), (amount // 2,), 0, 1 << 20) % (margin + 1)
    lengths = lengths.at[giver].add(-moved).at[taker].add(moved)
    members = jnp.searchsorted(jnp.cumsum(lengths), jnp.arange(rows * top), side="right").astype(jnp.int32)
    grid = members.reshape(top, rows).T
    grid = grid[jax.random.permutation(jax.random.fold_in(own, 1), rows)]
    offset_by = jax.random.randint(jax.random.fold_in(own, 2), (rows, 1), 0, top)
    return jnp.take_along_axis(grid, (jnp.arange(top)[None, :] + offset_by) % top, axis=1)


def portions_of(count, total, limit, lean, full):
    weights = [(1 << 20) // math.isqrt(standing ** lean) + 1 for standing in range(1, count + 1)]
    largest = limit if full else min(limit, max(-(-total // count), total * weights[0] // sum(weights)))
    least = 1 if total - largest >= count - 1 else 0
    holding, spare = [largest] + [least] * (count - 1), total - largest - least * (count - 1)
    while spare > 0:
        candidates = [i for i in range(1, count) if holding[i] < largest] or [i for i in range(1, count) if holding[i] < limit]
        pool, left = sum([weights[i] for i in candidates]), spare
        for i in candidates:
            more = min(limit - holding[i], max(1, left * weights[i] // pool), spare)
            holding[i] = holding[i] + more
            spare = spare - more
    return np.array(holding)


def scatter_about(key, shape, scale, limit, cuts=(), kind=jnp.bfloat16):
    gain = level_of(key, shape, cuts, -0.22, 0.18) if cuts else 1.0
    entries = jax.random.normal(key, shape, jnp.float32) * scale * gain
    return jnp.minimum(jnp.maximum(entries, -limit), limit).astype(kind)


def setup_inputs(seed: int = 0) -> dict:
    streams_of = jax.random.split(jax.random.key(seed), 7)
    tokens = scatter_about(streams_of[0], (TOKENS, D), 1.0, 6.0, ((0, 16), (1, 8)))
    input_weight = scatter_about(streams_of[1], (3, D, D), D ** -0.5, 0.0625, ((1, 16), (2, 8)))
    filter_taps = scatter_about(streams_of[2], (FLT, D), 0.15, 0.9, ((1, 8),), jnp.float32)
    decay_rates = jnp.clip(jnp.exp(math.log(0.3) - 4.6051702 * jax.random.uniform(streams_of[3], (D,), jnp.float32) ** level_of(streams_of[3], (D,), ((0, 8),), -0.2, 0.2)), 0.003, 0.3)
    skip_gain = jnp.clip(1.0 + 0.1 * jax.random.normal(streams_of[4], (D,), jnp.float32), 0.5, 1.5)
    owners_keys = jax.random.split(jax.random.fold_in(streams_of[5], 1), PAGES // PAGES_DEV)
    owners_turns = jax.random.permutation(jax.random.fold_in(streams_of[5], 3), PAGES // PAGES_DEV)
    owners = jax.vmap(lambda own, number: assign_block(jax.random.fold_in(streams_of[5], 2), own, number, PAGES_DEV, N_SEQ, 1, CAP, 2))(owners_keys, owners_turns).reshape((PAGES, 1))
    return dict(tokens=tokens, input_weight=input_weight, filter_taps=filter_taps, decay_rates=decay_rates, skip_gain=skip_gain, owners=owners)


def causal_filter(u_float, taps):
    rows = u_float.shape[0]
    padded = jnp.concatenate([jnp.zeros((FLT - 1, u_float.shape[1]), u_float.dtype), u_float], axis=0)

    def add_group(group, total):
        for inner in range(8):
            lag = group * 8 + inner
            start = (FLT - 1 - lag).astype(jnp.int32)
            shifted = lax.dynamic_slice_in_dim(padded, start, rows, 0)
            weight_row = lax.dynamic_slice_in_dim(taps, lag.astype(jnp.int32), 1, 0)
            total = total + weight_row * shifted
        return total

    return lax.fori_loop(0, FLT // 8, add_group, jnp.zeros_like(u_float))


def reference(tokens, input_weight, filter_taps, decay_rates, skip_gain, owners):
    projected_inputs = []
    for index in range(3):
        projected_inputs.append(jnp.dot(tokens, input_weight[index], preferred_element_type=jnp.float32).astype(jnp.bfloat16))
    query, key_part, value_slice = projected_inputs
    u_values = (key_part.astype(jnp.float32) * value_slice.astype(jnp.float32)).astype(jnp.bfloat16)
    lags = jnp.arange(FLT, dtype=jnp.float32)
    taps = filter_taps * jnp.exp(-decay_rates[None, :] * lags[:, None])
    u_float = u_values.astype(jnp.float32)
    mixed = causal_filter(u_float, taps) + skip_gain[None, :] * u_float
    gated = (query.astype(jnp.float32) * mixed).astype(jnp.bfloat16)

    rows_per_page = u_values.reshape(PAGES, PAGE_ROWS, D)
    owner = owners[:, 0].astype(jnp.int32)
    onehot = (owner[:, None] == jnp.arange(N_SEQ, dtype=jnp.int32)[None, :]).astype(jnp.int32)
    blocks = onehot.reshape(N_SEQ, PAGES_DEV, N_SEQ)
    earlier = jnp.cumsum(blocks, axis=1) - blocks
    slot = jnp.sum(earlier * blocks, axis=2).reshape(PAGES).astype(jnp.int32)
    source = (jnp.arange(PAGES, dtype=jnp.int32) // PAGES_DEV).astype(jnp.int32)
    target = (owner * (N_SEQ * CAP) + source * CAP + slot).astype(jnp.int32)
    handed = jnp.zeros((N_SEQ * N_SEQ * CAP, PAGE_ROWS, D), jnp.bfloat16).at[target].set(rows_per_page)
    return gated, handed
```

```python
import jax
import jax.numpy as jnp
from jax import lax
from jax.experimental import pallas as pl
from jax.experimental.pallas import tpu as pltpu
from jax.sharding import PartitionSpec as P

MESH = pl.DeviceIdType.MESH
F32, BF16 = jnp.float32, jnp.bfloat16
CHUNKS, LANES = 8, 128
ROWS, HALF = 256, 512
WINDOW = 3


def kernel(tok, wgt, taps_in, decay, skip, owners, gated, handed,
           wbuf, tbuf, own, osend, orecv, qbuf, ubuf, hrecv, psend, pbuf, sel, taps, shifts,
           wl, ws, wr, tzs, tzr, tys, tyr, os_, or_, hs, hr, ps, pr):
    s, c = lax.axis_index("seq"), lax.axis_index("chan")
    core, x, zh = s % 2, (s // 2) % 4, s // 8
    zl, y = c // 4, c % 4

    def dev(zh_, x_, core_, zl_, y_):
        return ((zh_ * 4 + x_) * 2 + core_, zl_ * 4 + y_)

    def remote(src, dst, ss, rs, to):
        return pltpu.make_async_remote_copy(
            src_ref=src, dst_ref=dst, send_sem=ss, recv_sem=rs, device_id=to, device_id_type=MESH)

    def kb(dx):
        return ((x + dx) % 4) * 2 + core

    def load(j):
        return pltpu.make_async_copy(
            wgt.at[:, :, pl.ds(pl.multiple_of(j * LANES, LANES), LANES)], wbuf.at[j, kb(0)], wl.at[j])

    @pl.loop(0, CHUNKS)
    def _(j):
        load(j).start()

    barrier = pltpu.get_barrier_semaphore()

    @pl.loop(1, 16)
    def _(o):
        pl.semaphore_signal(barrier, inc=1, device_id=((s + o) % 16, c), device_id_type=MESH)

    for dy in (1, 2, 3):
        pl.semaphore_signal(barrier, inc=1, device_id=dev(zh, x, core, zl, (y + dy) % 4), device_id_type=MESH)
    for z in (0, 1):
        pl.semaphore_signal(barrier, inc=1, device_id=dev(z, x, core, 1 - zl, y), device_id_type=MESH)
    pl.semaphore_wait(barrier, 20)

    def w_plus(j):
        return remote(wbuf.at[j, kb(0)], wbuf.at[j, kb(0)], ws.at[0, j], wr.at[0, j], dev(zh, (x + 1) % 4, core, zl, y))

    def w_minus(j):
        return remote(wbuf.at[j, kb(0)], wbuf.at[j, kb(0)], ws.at[1, j], wr.at[1, j], dev(zh, (x + 3) % 4, core, zl, y))

    def w_far(j):
        way = 1 + 2 * (j % 2)
        block = wbuf.at[j, ((x + 4 - way) % 4) * 2 + core]
        return remote(block, block, ws.at[2, j], wr.at[2, j], dev(zh, (x + way) % 4, core, zl, y))

    def w_pair(j, q):
        block = wbuf.at[j, ((x + q) % 4) * 2 + core]
        return remote(block, block, ws.at[3 + q, j], wr.at[3 + q, j], dev(zh, x, 1 - core, zl, y))

    def w_send(j):
        load(j).wait()
        w_plus(j).start()
        w_minus(j).start()
        w_pair(j, 0).start()

    def t_z(d):
        return remote(tok, tbuf.at[y, zh], tzs.at[d], tzr.at[zh], dev(zl, x, core, d, y))

    def t_own():
        return pltpu.make_async_copy(tok, tbuf.at[y, zh], tzr.at[zh])

    for d in (0, 1):
        stays = jnp.logical_and(zl == zh, zl == d)

        @pl.when(stays)
        def _():
            t_own().start()

        @pl.when(jnp.logical_not(stays))
        def _():
            t_z(d).start()

    @pl.loop(0, WINDOW)
    def _(j):
        w_send(j)

    def t_y(r, dy):
        return remote(tbuf.at[y, r], tbuf.at[y, r], tys.at[r, dy - 1], tyr.at[r, dy - 1],
                      dev(zh, x, core, zl, (y + dy) % 4))

    lag = lax.broadcasted_iota(jnp.int32, (128, LANES), 0)
    for j in range(CHUNKS):
        cols = slice(j * LANES, (j + 1) * LANES)
        value = taps_in[:, cols] * jnp.exp(-decay[:, cols] * lag.astype(F32))
        taps[j] = value + jnp.where(lag == 0, skip[:, cols], 0.0)
    iota = lambda shape, axis: lax.broadcasted_iota(jnp.int32, shape, axis)
    dot = lambda a, b, dims: lax.dot_general(a, b, (dims, ((), ())), preferred_element_type=F32)
    names = jnp.broadcast_to(owners[...], (32, 128))
    onehot = (names == iota((32, 128), 1)).astype(F32)
    before = (iota((32, 32), 1) < iota((32, 32), 0)).astype(BF16)
    earlier = dot(before, onehot.astype(BF16), ((1,), (0,)))
    slot = jnp.sum(earlier * onehot, axis=1, keepdims=True)
    target = owners[...].astype(F32) * 2.0 + slot
    place = (jnp.broadcast_to(target, (32, 32)) == iota((32, 32), 1).astype(F32)).astype(BF16)
    spread = (iota((ROWS, 32), 0) // 8 == iota((ROWS, 32), 1)).astype(BF16)
    part = dot(spread, place, ((1,), (1,))).astype(BF16)
    whole = dot(part, spread, ((1,), (1,)))
    same = (iota((ROWS, ROWS), 0) % 8 == iota((ROWS, ROWS), 1) % 8).astype(F32)
    sel[...] = (whole * same).astype(BF16)

    for r in (0, 1):
        pltpu.make_async_copy(tbuf.at[y, r], tbuf.at[y, r], tzr.at[r]).wait()
        for dy in (1, 3, 2):
            t_y(r, dy).start()

    def o_copy(j):
        return remote(osend.at[j], orecv.at[j], os_.at[j], or_.at[j], dev(1 - zh, x, core, zl, y))

    def h_copy(j):
        after = (s + 1) % 16
        return remote(ubuf.at[j, pl.ds(128, 128)], hrecv.at[j], hs.at[j], hr.at[j], (after, c))

    def p_copy(j, o):
        to = (s + o) % 16
        return remote(psend.at[j, pl.ds(pl.multiple_of(to * 16, 16), 16)],
                      pbuf.at[j, pl.ds(pl.multiple_of(s * 16, 16), 16)], ps.at[j], pr.at[j], (to, c))

    def matmul(j, row):
        def add(xx, total):
            for half in (0, 1):
                w = jnp.concatenate([wbuf[j, xx * 2 + half, p] for p in range(3)], axis=1)
                total = total + jnp.dot(tbuf[xx, row, :, half * HALF:(half + 1) * HALF], w,
                                        preferred_element_type=F32)
            return total
        return lax.fori_loop(0, 4, add, jnp.zeros((ROWS, 3 * LANES), F32))

    def stage_mm(j):
        for q in range(4):
            w_pair(j, q).wait_recv()
        osend[j] = matmul(j, 1 - zh).astype(BF16)
        o_copy(j).start()
        own[j % 2] = matmul(j, zh)

    def stage_u(j):
        o_copy(j).wait_recv()
        full = (own[j % 2] + orecv[j].astype(F32)).astype(BF16)
        qbuf[j] = full[:, :LANES]
        u = (full[:, LANES:2 * LANES].astype(F32) * full[:, 2 * LANES:].astype(F32)).astype(BF16)
        ubuf[j] = u
        h_copy(j).start()
        psend[j] = jnp.dot(sel[...], u, preferred_element_type=F32).astype(BF16)

        @pl.loop(1, 16)
        def _(o):
            p_copy(j, o).start()

        mine = pl.ds(pl.multiple_of(s * 16, 16), 16)
        handed[mine, pl.ds(pl.multiple_of(j * LANES, LANES), LANES)] = psend[j, mine]

    def stage_filter(j):
        h_copy(j).wait_recv()
        u = ubuf[j].astype(F32)
        prior = jnp.where(s == 0, 0.0, hrecv[j].astype(F32))
        ext = jnp.concatenate([prior, u], axis=0)
        for b in range(8):
            shifts[b] = ext[8 - b:384 - b]

        def add(a, total):
            rows = taps[j, pl.ds(pl.multiple_of(a * 8, 8), 8)]
            at = pl.multiple_of(120 - a * 8, 8)
            for b in range(8):
                total = total + rows[b:b + 1] * shifts[b, pl.ds(at, ROWS)]
            return total

        z = lax.fori_loop(0, 16, add, jnp.zeros((ROWS, LANES), F32))
        gated[:, pl.ds(pl.multiple_of(j * LANES, LANES), LANES)] = (qbuf[j].astype(F32) * z).astype(BF16)

    def tick(t):
        @pl.when(t < CHUNKS)
        def _():
            stage_mm(t)

        @pl.when(jnp.logical_and(t >= 1, t <= CHUNKS))
        def _():
            stage_u(t - 1)

        @pl.when(t >= 2)
        def _():
            stage_filter(t - 2)

    def reached(i):
        return jnp.where(i < 5, 0, jnp.where(i >= 8, 10, (i - 4) * 2))

    @pl.loop(0, CHUNKS + 1)
    def _(i):
        @pl.when(i + WINDOW < CHUNKS)
        def _():
            w_send(i + WINDOW)

        @pl.when(i < CHUNKS)
        def _():
            w_plus(i).wait_recv()
            w_minus(i).wait_recv()
            w_far(i).start()
            w_pair(i, 1).start()
            w_pair(i, 3).start()

        @pl.when(i >= 1)
        def _():
            w_far(i - 1).wait_recv()
            w_pair(i - 1, 2).start()

        @pl.when(i == 5)
        def _():
            for r in (0, 1):
                for dy in (1, 3, 2):
                    t_y(r, dy).wait_recv()

        @pl.loop(reached(i - 1), reached(i))
        def _(t):
            tick(t)

    @pl.loop(0, CHUNKS)
    def _(j):
        some = pbuf.at[j, pl.ds(0, 240)]
        pltpu.make_async_copy(some, some, pr.at[j]).wait()
        pltpu.make_async_copy(some, some, ps.at[j]).wait()

        @pl.loop(1, 16)
        def _(o):
            rows = pl.ds(pl.multiple_of(((s + o) % 16) * 16, 16), 16)
            handed[rows, pl.ds(pl.multiple_of(j * LANES, LANES), LANES)] = pbuf[j, rows]

        w_plus(j).wait_send()
        w_minus(j).wait_send()
        w_far(j).wait_send()
        for q in range(4):
            w_pair(j, q).wait_send()
        o_copy(j).wait_send()
        h_copy(j).wait_send()

    for r in (0, 1):
        for dy in (1, 2, 3):
            t_y(r, dy).wait_send()
    for d in (0, 1):
        @pl.when(jnp.logical_not(jnp.logical_and(zl == zh, zl == d)))
        def _():
            t_z(d).wait_send()


def per_device(tokens, input_weight, filter_taps, decay_rates, skip_gain, owners):
    dma = pltpu.SemaphoreType.DMA
    vmem, any_ = pl.BlockSpec(memory_space=pltpu.VMEM), pl.BlockSpec(memory_space=pl.ANY)
    gated, handed = pl.pallas_call(
        kernel,
        out_shape=(jax.ShapeDtypeStruct((ROWS, 1024), BF16), jax.ShapeDtypeStruct((ROWS, 1024), BF16)),
        in_specs=[any_, any_, vmem, vmem, vmem, vmem],
        out_specs=(vmem, vmem),
        scratch_shapes=[
            pltpu.VMEM((CHUNKS, 8, 3, HALF, LANES), BF16),
            pltpu.VMEM((4, 2, ROWS, 1024), BF16),
            pltpu.VMEM((2, ROWS, 3 * LANES), F32),
            pltpu.VMEM((CHUNKS, ROWS, 3 * LANES), BF16),
            pltpu.VMEM((CHUNKS, ROWS, 3 * LANES), BF16),
            pltpu.VMEM((CHUNKS, ROWS, LANES), BF16),
            pltpu.VMEM((CHUNKS, ROWS, LANES), BF16),
            pltpu.VMEM((CHUNKS, 128, LANES), BF16),
            pltpu.VMEM((CHUNKS, ROWS, LANES), BF16),
            pltpu.VMEM((CHUNKS, ROWS, LANES), BF16),
            pltpu.VMEM((ROWS, ROWS), BF16),
            pltpu.VMEM((CHUNKS, 128, LANES), F32),
            pltpu.VMEM((8, 376, LANES), F32),
            dma((CHUNKS,)), dma((7, CHUNKS)), dma((7, CHUNKS)),
            dma((2,)), dma((2,)), dma((2, 3)), dma((2, 3)),
            dma((CHUNKS,)), dma((CHUNKS,)), dma((CHUNKS,)), dma((CHUNKS,)), dma((CHUNKS,)), dma((CHUNKS,)),
        ],
        compiler_params=pltpu.CompilerParams(
            collective_id=0, has_side_effects=True, vmem_limit_bytes=56 * 1024 * 1024),
        name="hyena",
    )(tokens, input_weight, filter_taps, decay_rates.reshape(1, -1), skip_gain.reshape(1, -1), owners)
    return gated, handed.reshape(32, 8, 1024)


def solution(mesh):
    return jax.shard_map(
        per_device,
        mesh=mesh,
        in_specs=(P("seq", "chan"), P(None, "seq", "chan"), P(None, "chan"), P("chan"), P("chan"), P("seq", None)),
        out_specs=(P("seq", "chan"), P("seq", None, "chan")),
        check_vma=False,
    )
```

```python
import jax
import jax.numpy as jnp
from jax import lax
from jax.experimental import pallas as pl
from jax.experimental.pallas import tpu as pltpu
from jax.sharding import PartitionSpec as P

MESH = pl.DeviceIdType.MESH
F32, BF16 = jnp.float32, jnp.bfloat16
CHUNKS, LANES = 4, 128
ROWS, HALF, SUB = 256, 512, 128
MESSAGES = 8


def kernel(tok, wgt, taps_in, decay, skip, owners, gated, handed,
           wbuf, wother, tbuf, txbuf, osend, orecv, qbuf, ubuf, hrecv, psend, pbuf, gsend, grecv,
           mine, theirs, sel, taps, shifts,
           wl, ws, wr, txs, txr, tzs, tzr, tys, tyr, os_, or_, hs, hr, ps, pr, gs, gr, ms, mr):
    s, c = lax.axis_index("seq"), lax.axis_index("chan")
    core, x, zh = s % 2, (s // 2) % 4, s // 8
    zl, y = c // 4, c % 4
    zo, x2 = 1 - zh, (x + 2) % 4

    def dev(zh_, x_, core_, zl_, y_):
        return ((zh_ * 4 + x_) * 2 + core_, zl_ * 4 + y_)

    def remote(src, dst, ss, rs, to):
        return pltpu.make_async_remote_copy(
            src_ref=src, dst_ref=dst, send_sem=ss, recv_sem=rs, device_id=to, device_id_type=MESH)

    def at(start, size):
        return pl.ds(pl.multiple_of(start * size, size), size)

    def group(j):
        return ((x + j % 2) // 2) % 2

    def beside(j):
        up = 1 - 2 * ((x + j) % 2)
        return (x + 4 + up) % 4

    def across(j):
        up = 1 - 2 * ((x + j + 1) % 2)
        return (x + 4 + up) % 4

    def kb(xx):
        return xx * 2 + core

    def load(j):
        return pltpu.make_async_copy(wgt.at[:, :, at(2 * j + group(j), LANES)], wbuf.at[j, kb(x)], wl.at[0, j])

    def load_other(j):
        return pltpu.make_async_copy(wgt.at[:, :, at(2 * j + 1 - group(j), LANES)], wother.at[j], wl.at[1, j])

    @pl.loop(0, CHUNKS)
    def _(j):
        load(j).start()
        load_other(j).start()

    barrier = pltpu.get_barrier_semaphore()

    @pl.loop(1, 16)
    def _(o):
        pl.semaphore_signal(barrier, inc=1, device_id=((s + o) % 16, c), device_id_type=MESH)

    for dy in (1, 2, 3):
        pl.semaphore_signal(barrier, inc=1, device_id=dev(zh, x, core, zl, (y + dy) % 4), device_id_type=MESH)
    for z in (0, 1):
        pl.semaphore_signal(barrier, inc=1, device_id=dev(z, x, core, 1 - zl, y), device_id_type=MESH)
    pl.semaphore_wait(barrier, 20)

    def w_beside(j):
        return remote(wbuf.at[j, kb(x)], wbuf.at[j, kb(x)], ws.at[0, j], wr.at[0, j], dev(zh, beside(j), core, zl, y))

    def w_across(j):
        return remote(wother.at[j], wbuf.at[j, kb(x)], ws.at[1, j], wr.at[1, j], dev(zh, across(j), core, zl, y))

    def w_far(j):
        block = wbuf.at[j, kb(across(j))]
        return remote(block, block, ws.at[2, j], wr.at[2, j], dev(zh, beside(j), core, zl, y))

    def w_pair(j, k):
        block = wbuf.at[j, kb((x + k) % 4)]
        return remote(block, block, ws.at[3 + k, j], wr.at[3 + k, j], dev(zh, x, 1 - core, zl, y))

    def w_send(j):
        load(j).wait()
        load_other(j).wait()
        w_beside(j).start()
        w_across(j).start()
        w_pair(j, 0).start()

    def t_x(sub):
        return remote(tok.at[at(sub, SUB)], txbuf.at[at(sub, SUB)], txs.at[sub], txr.at[sub], dev(zh, x2, core, zl, y))

    def t_z(e, sub, d):
        src = txbuf if e else tok
        return remote(src.at[at(sub, SUB)], tbuf.at[y, zh, e, at(sub, SUB)], tzs.at[e, sub, d], tzr.at[zh, e, sub],
                      dev(zl, x, core, d, y))

    def t_own(e, sub):
        src = txbuf if e else tok
        return pltpu.make_async_copy(src.at[at(sub, SUB)], tbuf.at[y, zh, e, at(sub, SUB)], tzr.at[zh, e, sub])

    def stays(d):
        return jnp.logical_and(zl == zh, zl == d)

    def t_along_z(e, sub):
        for d in (0, 1):
            @pl.when(stays(d))
            def _():
                t_own(e, sub).start()

            @pl.when(jnp.logical_not(stays(d)))
            def _():
                t_z(e, sub, d).start()

    def block_of(m):
        r = m // 2
        return jnp.where(r < 2, zo, zh), jnp.where((r == 1) | (r == 2), 1, 0)

    def t_piece(yy, m):
        z, e = block_of(m)
        return tbuf.at[yy, z, e, at(m % 2, SUB)]

    def t_near(m, k):
        piece = t_piece(y, m)
        return remote(piece, piece, tys.at[k, m], tyr.at[k, m], dev(zh, x, core, zl, (y + 1 + 2 * k) % 4))

    def t_next(m, k):
        z, e = block_of(m)
        piece = tbuf.at[(y + 3 - 2 * k) % 4, z, e, at((m % 2) * 2 + k, SUB // 2)]
        return remote(piece, piece, tys.at[2 + k, m], tyr.at[2 + k, m], dev(zh, x, core, zl, (y + 1 + 2 * k) % 4))

    def t_along_y(m):
        z, e = block_of(m)
        piece = t_piece(y, m)
        pltpu.make_async_copy(piece, piece, tzr.at[z, e, m % 2]).wait()
        t_near(m, 0).start()
        t_near(m, 1).start()

    for sub in (0, 1):
        t_x(sub).start()
        t_along_z(0, sub)

    w_send(0)
    w_send(1)

    iota = lambda shape, axis: lax.broadcasted_iota(jnp.int32, shape, axis)
    dot = lambda a, b, dims: lax.dot_general(a, b, (dims, ((), ())), preferred_element_type=F32)
    names = jnp.broadcast_to(owners[...], (32, 128))
    onehot = (names == iota((32, 128), 1)).astype(F32)
    before = (iota((32, 32), 1) < iota((32, 32), 0)).astype(BF16)
    earlier = dot(before, onehot.astype(BF16), ((1,), (0,)))
    slot = jnp.sum(earlier * onehot, axis=1, keepdims=True)
    mine[...] = jnp.broadcast_to(owners[...].astype(F32) * 2.0 + slot, (32, 128)).astype(BF16)

    def m_copy():
        return remote(mine, theirs, ms, mr, dev(zh, x2, core, zl, y))

    m_copy().start()
    t_along_y(0)
    t_x(0).wait_recv()
    t_along_z(1, 0)
    t_along_y(1)
    t_x(1).wait_recv()
    t_along_z(1, 1)

    def order(target):
        place = (target[:, :32].astype(F32) == iota((32, 32), 1).astype(F32)).astype(BF16)
        spread = (iota((ROWS, 32), 0) // 8 == iota((ROWS, 32), 1)).astype(BF16)
        part = dot(spread, place, ((1,), (1,))).astype(BF16)
        whole = dot(part, spread, ((1,), (1,)))
        same = (iota((ROWS, ROWS), 0) % 8 == iota((ROWS, ROWS), 1) % 8).astype(F32)
        return (whole * same).astype(BF16)

    sel[0] = order(mine[...])
    m_copy().wait_recv()
    sel[1] = order(theirs[...])

    lag = iota((128, LANES), 0)

    @pl.loop(0, CHUNKS)
    def _(j):
        cols = at(2 * j + group(j), LANES)
        value = taps_in[:, cols] * jnp.exp(-decay[:, cols] * lag.astype(F32))
        taps[j] = value + jnp.where(lag == 0, skip[:, cols], 0.0)

    def matmul(j, z, e):
        def add(xx, total):
            for half in (0, 1):
                w = jnp.concatenate([wbuf[j, xx * 2 + half, p] for p in range(3)], axis=1)
                total = total + jnp.dot(tbuf[xx, z, e, :, half * HALF:(half + 1) * HALF], w,
                                        preferred_element_type=F32)
            return total
        return lax.fori_loop(0, 4, add, jnp.zeros((ROWS, 3 * LANES), F32))

    def o_copy(j, e):
        return remote(osend.at[j, e], orecv.at[j, e], os_.at[j, e], or_.at[j, e], dev(zo, x, core, zl, y))

    def h_copy(j, e):
        xe = (x + 2 * e) % 4
        to = beside(j)
        same = jnp.where((xe + 1) % 4 == to, 0, 1)
        to_x, to_zh = jnp.where(core == 0, x, to), jnp.where(core == 0, zh, (zh + xe // 3) % 2)
        to_e = jnp.where(core == 0, e, same)
        return remote(ubuf.at[j, e, pl.ds(128, 128)], hrecv.at[j, to_e], hs.at[j, e], hr.at[j, to_e],
                      dev(to_zh, to_x, 1 - core, zl, y))

    def p_copy(j, e, o):
        to, source = (s + o) % 16, (zh * 4 + (x + 2 * e) % 4) * 2 + core
        return remote(psend.at[j, e, at(to, 16)], pbuf.at[2 * j + group(j), at(source, 16)],
                      ps.at[j, e], pr.at[2 * j + group(j)], (to, c))

    def g_copy(j):
        return remote(gsend.at[j], grecv.at[j], gs.at[j], gr.at[j], dev(zh, x2, core, zl, y))

    def stage_other(n):
        e = jnp.where(n < 6, n // 3, n - 6)
        j = jnp.where(n < 6, n % 3, 3)
        osend[j, e] = matmul(j, zo, e).astype(BF16)
        o_copy(j, e).start()

    def stage_u(j, e):
        own = matmul(j, zh, e)
        o_copy(j, e).wait_recv()
        full = (own + orecv[j, e].astype(F32)).astype(BF16)
        qbuf[j, e] = full[:, :LANES]
        u = (full[:, LANES:2 * LANES].astype(F32) * full[:, 2 * LANES:].astype(F32)).astype(BF16)
        ubuf[j, e] = u
        h_copy(j, e).start()
        psend[j, e] = jnp.dot(sel[e], u, preferred_element_type=F32).astype(BF16)

        @pl.loop(1, 16)
        def _(o):
            p_copy(j, e, o).start()

        source = (zh * 4 + (x + 2 * e) % 4) * 2 + core
        pbuf[2 * j + group(j), at(source, 16)] = psend[j, e, at(s, 16)]

    def stage_filter(j, e):
        pltpu.make_async_copy(hrecv.at[j, e], hrecv.at[j, e], hr.at[j, e]).wait()
        first = (zh == 0) & (core == 0) & ((x + 2 * e) % 4 == 0)
        prior = jnp.where(first, 0.0, hrecv[j, e].astype(F32))
        ext = jnp.concatenate([prior, ubuf[j, e].astype(F32)], axis=0)
        for b in range(8):
            shifts[b] = ext[8 - b:384 - b]

        def add(a, total):
            rows = taps[j, at(a, 8)]
            for b in range(8):
                total = total + rows[b:b + 1] * shifts[b, pl.ds(pl.multiple_of(120 - a * 8, 8), ROWS)]
            return total

        z = lax.fori_loop(0, 16, add, jnp.zeros((ROWS, LANES), F32))
        out = (qbuf[j, e].astype(F32) * z).astype(BF16)

        @pl.when(e == 1)
        def _():
            gsend[j] = out
            g_copy(j).start()

        @pl.when(e == 0)
        def _():
            gated[:, at(2 * j + group(j), LANES)] = out

    def others_done(i):
        return jnp.where(i < 2, 0, jnp.where(i < 4, i - 1, jnp.where(i == 4, 6, 8)))

    @pl.loop(0, MESSAGES + 1)
    def _(i):
        @pl.when((i >= 1) & (i <= 4))
        def _():
            j = i - 1
            w_across(j).wait_recv()
            w_far(j).start()
            w_pair(j, (across(j) + 4 - x) % 4).start()
            w_beside(j).wait_recv()
            w_pair(j, (beside(j) + 4 - x) % 4).start()

            @pl.when(j + 2 < CHUNKS)
            def _():
                w_send(j + 2)

        @pl.when(i < MESSAGES)
        def _():
            t_near(i, 0).wait_recv()
            t_next(i, 0).start()
            t_near(i, 1).wait_recv()
            t_next(i, 1).start()

        @pl.when(i + 2 < MESSAGES)
        def _():
            t_along_y(i + 2)

        @pl.when((i >= 2) & (i <= 5))
        def _():
            w_far(i - 2).wait_recv()
            w_pair(i - 2, 2).start()

        @pl.when(i >= 1)
        def _():
            t_next(i - 1, 0).wait_recv()
            t_next(i - 1, 1).wait_recv()

        @pl.when((i >= 2) & (i <= 5))
        def _():
            for k in range(4):
                w_pair(i - 2, k).wait_recv()

        @pl.loop(others_done(i - 1), others_done(i))
        def _(n):
            stage_other(n)

        @pl.when((i == 6) | (i == 8))
        def _():
            @pl.loop(0, jnp.where(i == 6, 4, 9))
            def _(t):
                @pl.when(t < 4)
                def _():
                    stage_u(t, jnp.where(i == 6, 1, 0))

                @pl.when((i == 8) & (t >= 1))
                def _():
                    stage_filter((t - 1) % 4, jnp.where(t <= 4, 1, 0))

    @pl.loop(0, CHUNKS)
    def _(j):
        few = pbuf.at[0, pl.ds(0, 224)]
        some = pbuf.at[0, pl.ds(0, 240)]
        all_ = pbuf.at[0]
        this, that = 2 * j + group(j), 2 * j + 1 - group(j)
        pltpu.make_async_copy(few, few, pr.at[this]).wait()
        pltpu.make_async_copy(all_, all_, pr.at[that]).wait()
        handed[:, at(this, LANES)] = pbuf[this]
        handed[:, at(that, LANES)] = pbuf[that]
        g_copy(j).wait_recv()
        gated[:, at(that, LANES)] = grecv[j]
        g_copy(j).wait_send()
        for e in (0, 1):
            pltpu.make_async_copy(some, some, ps.at[j, e]).wait()
            o_copy(j, e).wait_send()
            h_copy(j, e).wait_send()
        w_beside(j).wait_send()
        w_across(j).wait_send()
        w_far(j).wait_send()
        for k in range(4):
            w_pair(j, k).wait_send()

    @pl.loop(0, MESSAGES)
    def _(m):
        for k in (0, 1):
            t_near(m, k).wait_send()
            t_next(m, k).wait_send()

    m_copy().wait_send()
    for sub in (0, 1):
        t_x(sub).wait_send()
        for d in (0, 1):
            @pl.when(jnp.logical_not(stays(d)))
            def _():
                t_z(0, sub, d).wait_send()
                t_z(1, sub, d).wait_send()


def per_device(tokens, input_weight, filter_taps, decay_rates, skip_gain, owners):
    dma = pltpu.SemaphoreType.DMA
    vmem, any_ = pl.BlockSpec(memory_space=pltpu.VMEM), pl.BlockSpec(memory_space=pl.ANY)
    gated, handed = pl.pallas_call(
        kernel,
        out_shape=(jax.ShapeDtypeStruct((ROWS, 1024), BF16), jax.ShapeDtypeStruct((ROWS, 1024), BF16)),
        in_specs=[any_, any_, vmem, vmem, vmem, vmem],
        out_specs=(vmem, vmem),
        scratch_shapes=[
            pltpu.VMEM((CHUNKS, 8, 3, HALF, LANES), BF16),
            pltpu.VMEM((CHUNKS, 3, HALF, LANES), BF16),
            pltpu.VMEM((4, 2, 2, ROWS, 1024), BF16),
            pltpu.VMEM((ROWS, 1024), BF16),
            pltpu.VMEM((CHUNKS, 2, ROWS, 3 * LANES), BF16),
            pltpu.VMEM((CHUNKS, 2, ROWS, 3 * LANES), BF16),
            pltpu.VMEM((CHUNKS, 2, ROWS, LANES), BF16),
            pltpu.VMEM((CHUNKS, 2, ROWS, LANES), BF16),
            pltpu.VMEM((CHUNKS, 2, 128, LANES), BF16),
            pltpu.VMEM((CHUNKS, 2, ROWS, LANES), BF16),
            pltpu.VMEM((2 * CHUNKS, ROWS, LANES), BF16),
            pltpu.VMEM((CHUNKS, ROWS, LANES), BF16),
            pltpu.VMEM((CHUNKS, ROWS, LANES), BF16),
            pltpu.VMEM((32, 128), BF16),
            pltpu.VMEM((32, 128), BF16),
            pltpu.VMEM((2, ROWS, ROWS), BF16),
            pltpu.VMEM((CHUNKS, 128, LANES), F32),
            pltpu.VMEM((8, 376, LANES), F32),
            dma((2, CHUNKS)), dma((7, CHUNKS)), dma((7, CHUNKS)),
            dma((2,)), dma((2,)), dma((2, 2, 2)), dma((2, 2, 2)),
            dma((4, MESSAGES)), dma((4, MESSAGES)),
            dma((CHUNKS, 2)), dma((CHUNKS, 2)), dma((CHUNKS, 2)), dma((CHUNKS, 2)),
            dma((CHUNKS, 2)), dma((2 * CHUNKS,)), dma((CHUNKS,)), dma((CHUNKS,)), dma, dma,
        ],
        compiler_params=pltpu.CompilerParams(
            collective_id=0, has_side_effects=True, vmem_limit_bytes=56 * 1024 * 1024),
        name="hyena",
    )(tokens, input_weight, filter_taps, decay_rates.reshape(1, -1), skip_gain.reshape(1, -1), owners)
    return gated, handed.reshape(32, 8, 1024)


def solution(mesh):
    return jax.shard_map(
        per_device,
        mesh=mesh,
        in_specs=(P("seq", "chan"), P(None, "seq", "chan"), P(None, "chan"), P("chan"), P("chan"), P("seq", None)),
        out_specs=(P("seq", "chan"), P("seq", None, "chan")),
        check_vma=False,
    )
```

```python
import jax
import jax.numpy as jnp
from jax import lax
from jax.experimental import pallas as pl
from jax.experimental.pallas import tpu as pltpu
from jax.sharding import PartitionSpec as P

MESH = pl.DeviceIdType.MESH
F32, BF16 = jnp.float32, jnp.bfloat16
CHUNKS, LANES = 4, 128
ROWS, HALF = 256, 512
PARTS = 4
SUB, MESSAGES = ROWS // PARTS, 4 * PARTS
AHEAD, UNITS, W_AHEAD, W_LEAD = 4, 3 * CHUNKS, 3, 1


def kernel(tok, wgt, taps_in, decay, skip, owners, gated, handed,
           wbuf, wother, tbuf, txbuf, own, osend, orecv, qbuf, ubuf, hrecv, psend, pbuf, gsend, grecv,
           mine, theirs, sel, taps, shifts,
           wl, ws, wr, txs, txr, tzs, tzr, tys, tyr, os_, or_, hs, hr, ps, pr, gs, gr, ms, mr):
    s, c = lax.axis_index("seq"), lax.axis_index("chan")
    core, x, zh = s % 2, (s // 2) % 4, s // 8
    zl, y = c // 4, c % 4
    zo, x2 = 1 - zh, (x + 2) % 4

    def dev(zh_, x_, core_, zl_, y_):
        return ((zh_ * 4 + x_) * 2 + core_, zl_ * 4 + y_)

    def remote(src, dst, ss, rs, to):
        return pltpu.make_async_remote_copy(
            src_ref=src, dst_ref=dst, send_sem=ss, recv_sem=rs, device_id=to, device_id_type=MESH)

    def at(start, size):
        return pl.ds(pl.multiple_of(start * size, size), size)

    def group(j):
        return ((x + j % 2) // 2) % 2

    def beside(j):
        up = 1 - 2 * ((x + j) % 2)
        return (x + 4 + up) % 4

    def across(j):
        up = 1 - 2 * ((x + j + 1) % 2)
        return (x + 4 + up) % 4

    def kb(xx):
        return xx * 2 + core

    def load(j):
        return pltpu.make_async_copy(wgt.at[:, :, at(2 * j + group(j), LANES)], wbuf.at[j, kb(x)], wl.at[0, j])

    def load_other(j):
        return pltpu.make_async_copy(wgt.at[:, :, at(2 * j + 1 - group(j), LANES)], wother.at[j], wl.at[1, j])

    @pl.loop(0, CHUNKS)
    def _(j):
        load(j).start()
        load_other(j).start()

    barrier = pltpu.get_barrier_semaphore()

    partners = [dev(zh, (x + d) % 4, core, zl, y) for d in (1, 2, 3)] + [dev(zh, x, 1 - core, zl, y)]
    partners += [dev(zo, x, core, zl, y), dev(zh, x, core, 1 - zl, y), dev(zo, x, core, 1 - zl, y)]
    partners += [dev(zh, x, core, zl, (y + d) % 4) for d in (1, 3)]
    for partner in partners:
        pl.semaphore_signal(barrier, inc=1, device_id=partner, device_id_type=MESH)
    pl.semaphore_wait(barrier, len(partners))

    def w_beside(v):
        block = wbuf.at[v // 3, kb(x), v % 3]
        return remote(block, block, ws.at[0, v], wr.at[0, v], dev(zh, beside(v // 3), core, zl, y))

    def w_across(v):
        return remote(wother.at[v // 3, v % 3], wbuf.at[v // 3, kb(x), v % 3], ws.at[1, v], wr.at[1, v],
                      dev(zh, across(v // 3), core, zl, y))

    def w_far(v):
        block = wbuf.at[v // 3, kb(across(v // 3)), v % 3]
        return remote(block, block, ws.at[2, v], wr.at[2, v], dev(zh, beside(v // 3), core, zl, y))

    def w_pair(j, k):
        block = wbuf.at[j, kb((x + k) % 4)]
        return remote(block, block, ws.at[3 + k, j], wr.at[3 + k, j], dev(zh, x, 1 - core, zl, y))

    def w_send(v):
        @pl.when(v % 3 == 0)
        def _():
            load(v // 3).wait()
            load_other(v // 3).wait()

        w_beside(v).start()
        w_across(v).start()

    def w_step(v):
        @pl.when(v < UNITS)
        def _():
            w_across(v).wait_recv()
            w_far(v).start()
            w_beside(v).wait_recv()

            @pl.when(v + W_AHEAD < UNITS)
            def _():
                w_send(v + W_AHEAD)

        @pl.when((v >= 1) & (v <= UNITS))
        def _():
            w_far(v - 1).wait_recv()

            @pl.when(v % 3 == 0)
            def _():
                for k in range(4):
                    w_pair(v // 3 - 1, k).start()

    def t_x(sub):
        return remote(tok.at[at(sub, SUB)], txbuf.at[at(sub, SUB)], txs.at[sub], txr.at[sub], dev(zh, x2, core, zl, y))

    def t_z(e, sub, d):
        src = txbuf if e else tok
        return remote(src.at[at(sub, SUB)], tbuf.at[y, zh, e, at(sub, SUB)], tzs.at[e, sub, d], tzr.at[zh, e, sub],
                      dev(zl, x, core, d, y))

    def t_own(e, sub):
        src = txbuf if e else tok
        return pltpu.make_async_copy(src.at[at(sub, SUB)], tbuf.at[y, zh, e, at(sub, SUB)], tzr.at[zh, e, sub])

    def stays(d):
        return jnp.logical_and(zl == zh, zl == d)

    def t_along_z(e, sub):
        for d in (0, 1):
            @pl.when(stays(d))
            def _():
                t_own(e, sub).start()

            @pl.when(jnp.logical_not(stays(d)))
            def _():
                t_z(e, sub, d).start()

    early = x // 2

    def block_of(m):
        r = m // PARTS
        return jnp.where(r < 2, zo, zh), jnp.where(r < 2, r, (early + r) % 2)

    def t_piece(yy, m):
        z, e = block_of(m)
        return tbuf.at[yy, z, e, at(m % PARTS, SUB)]

    def t_near(m, k):
        piece = t_piece(y, m)
        return remote(piece, piece, tys.at[k, m], tyr.at[k, m], dev(zh, x, core, zl, (y + 1 + 2 * k) % 4))

    def t_next(m, k):
        z, e = block_of(m)
        piece = tbuf.at[(y + 3 - 2 * k) % 4, z, e, at((m % PARTS) * 2 + k, SUB // 2)]
        return remote(piece, piece, tys.at[2 + k, m], tyr.at[2 + k, m], dev(zh, x, core, zl, (y + 1 + 2 * k) % 4))

    def t_along_y(m):
        z, e = block_of(m)
        piece = t_piece(y, m)
        pltpu.make_async_copy(piece, piece, tzr.at[z, e, m % PARTS]).wait()
        t_near(m, 0).start()
        t_near(m, 1).start()

    for sub in range(PARTS):
        t_x(sub).start()
    for sub in range(PARTS):
        t_along_z(0, sub)
    for v in range(W_AHEAD):
        w_send(v)

    iota = lambda shape, axis: lax.broadcasted_iota(jnp.int32, shape, axis)
    dot = lambda a, b, dims: lax.dot_general(a, b, (dims, ((), ())), preferred_element_type=F32)
    onehot = (jnp.broadcast_to(owners[...], (32, 32)) == iota((32, 32), 0)).astype(F32)
    before = (iota((32, 32), 0) < iota((32, 32), 1)).astype(BF16)
    earlier = dot(onehot.astype(BF16), before, ((1,), (0,)))
    target = owners[...].astype(F32) * 2.0 + jnp.sum(earlier * onehot, axis=0, keepdims=True)
    place = (jnp.broadcast_to(target, (32, 32)) == iota((32, 32), 0).astype(F32)).astype(F32)
    mine[...] = jnp.concatenate([place, jnp.zeros((32, 96), F32)], axis=1).astype(BF16)

    def m_copy():
        return remote(mine, theirs, ms, mr, dev(zh, x2, core, zl, y))

    m_copy().start()
    t_along_y(0)
    t_along_y(1)
    w_step(0)
    for sub in range(PARTS):
        t_x(sub).wait_recv()
        t_along_z(1, sub)
        if sub + 2 < AHEAD:
            t_along_y(sub + 2)
        if sub + 1 < W_LEAD:
            w_step(sub + 1)

    def order(place):
        spread = (iota((ROWS, 32), 0) // 8 == iota((ROWS, 32), 1)).astype(BF16)
        part = dot(spread, place[:, :32], ((1,), (0,))).astype(BF16)
        whole = dot(part, spread, ((1,), (1,)))
        same = (iota((ROWS, ROWS), 0) % 8 == iota((ROWS, ROWS), 1) % 8).astype(F32)
        return (whole * same).astype(BF16)

    sel[0] = order(mine[...])
    m_copy().wait_recv()
    sel[1] = order(theirs[...])

    lag = iota((128, LANES), 0)

    @pl.loop(0, CHUNKS)
    def _(j):
        cols = at(2 * j + group(j), LANES)
        value = taps_in[:, cols] * jnp.exp(-decay[:, cols] * lag.astype(F32))
        taps[j] = value + jnp.where(lag == 0, skip[:, cols], 0.0)

    def matmul(j, z, e):
        t = jnp.concatenate([tbuf[yy, z, e] for yy in range(4)], axis=1)
        w = jnp.concatenate([jnp.concatenate([wbuf[j, k, p] for k in range(8)], axis=0) for p in range(3)], axis=1)
        return jnp.dot(t, w, preferred_element_type=F32)

    def o_copy(j, e):
        return remote(osend.at[j, e], orecv.at[j, e], os_.at[j, e], or_.at[j, e], dev(zo, x, core, zl, y))

    def h_copy(j, e):
        xe = (x + 2 * e) % 4
        to = beside(j)
        same = jnp.where((xe + 1) % 4 == to, 0, 1)
        to_x, to_zh = jnp.where(core == 0, x, to), jnp.where(core == 0, zh, (zh + xe // 3) % 2)
        to_e = jnp.where(core == 0, e, same)
        return remote(ubuf.at[j, e, pl.ds(128, 128)], hrecv.at[j, to_e], hs.at[j, e], hr.at[j, to_e],
                      dev(to_zh, to_x, 1 - core, zl, y))

    def p_copy(j, e, o):
        to, source = (s + o) % 16, (zh * 4 + (x + 2 * e) % 4) * 2 + core
        return remote(psend.at[j, e, at(to, 16)], pbuf.at[2 * j + group(j), at(source, 16)],
                      ps.at[j, e], pr.at[2 * j + group(j)], (to, c))

    def g_copy(j):
        return remote(gsend.at[j], grecv.at[j], gs.at[j], gr.at[j], dev(zh, x2, core, zl, y))

    def stage_other(n):
        e = jnp.where(n < 2, 0, jnp.where(n < 4, 1, n % 2))
        j = jnp.where(n < 2, n, jnp.where(n < 4, n - 2, n // 2))
        osend[j, e] = matmul(j, zo, e).astype(BF16)
        o_copy(j, e).start()

    def stage_own(j, e):
        own[j] = matmul(j, zh, e)

    def stage_u(j, e):
        o_copy(j, e).wait_recv()
        full = (own[j] + orecv[j, e].astype(F32)).astype(BF16)
        qbuf[j, e] = full[:, :LANES]
        u = (full[:, LANES:2 * LANES].astype(F32) * full[:, 2 * LANES:].astype(F32)).astype(BF16)
        ubuf[j, e] = u
        h_copy(j, e).start()
        psend[j, e] = jnp.dot(sel[e], u, preferred_element_type=F32).astype(BF16)

        @pl.loop(1, 16)
        def _(o):
            p_copy(j, e, o).start()

        source = (zh * 4 + (x + 2 * e) % 4) * 2 + core
        pbuf[2 * j + group(j), at(source, 16)] = psend[j, e, at(s, 16)]

    def stage_filter(j, e):
        pltpu.make_async_copy(hrecv.at[j, e], hrecv.at[j, e], hr.at[j, e]).wait()
        first = (zh == 0) & (core == 0) & ((x + 2 * e) % 4 == 0)
        prior = jnp.where(first, 0.0, hrecv[j, e].astype(F32))
        ext = jnp.concatenate([prior, ubuf[j, e].astype(F32)], axis=0)
        for b in range(8):
            shifts[b] = ext[8 - b:384 - b]

        def stream(count, tap, data):
            def add(b, sums):
                x_ = [data(b, m) for m in range(count + 7)]
                sums = list(sums)
                for a in range(8):
                    weight = jnp.broadcast_to(tap(b, a), (8, LANES))
                    for r in range(count):
                        sums[r] = sums[r] + weight * x_[r - a + 7]
                return tuple(sums)
            return lax.fori_loop(0, 8, add, tuple(jnp.zeros((8, LANES), F32) for _ in range(count)), unroll=2)

        def rows_of(b, m):
            return shifts[b, 8 * m:8 * m + 8]

        def tap_of(b, a):
            return taps[j, pl.ds(8 * a + b, 1)]

        even = stream(16, lambda b, a: tap_of(b, 2 * a), lambda b, m: rows_of(b, 2 * m + 1))
        odd = stream(17, lambda b, a: tap_of(b, 2 * a + 1), lambda b, m: rows_of(b, 2 * m))
        both = stream(16, lambda b, a: tap_of(b, 2 * a) + tap_of(b, 2 * a + 1),
                      lambda b, m: rows_of(b, 2 * m + 1) + rows_of(b, 2 * m + 2))
        z = jnp.concatenate(
            [piece for r in range(16) for piece in (even[r] + odd[r], both[r] - even[r] - odd[r + 1])], axis=0)
        out = (qbuf[j, e].astype(F32) * z).astype(BF16)

        @pl.when(e == 1)
        def _():
            gsend[j] = out
            g_copy(j).start()

        @pl.when(e == 0)
        def _():
            gated[:, at(2 * j + group(j), LANES)] = out

    waits = (zh == 1) & (core == 0) & (x % 2 == 0)
    now = jnp.where(waits, 0, 3)

    def others_done(i):
        return jnp.where(i < 4, 0, jnp.where(i < 8, i // 2 - 1, jnp.where(i < 11, i - 4, jnp.where(i < 12, 6, 8))))

    def owns_done(i):
        return jnp.where(i < 13, 0, jnp.where(i == 13, 2, jnp.where(i < 16, 3, 8)))

    def filters_done(i):
        return jnp.where(i < 14, 0, jnp.where(i == 14, jnp.minimum(now, 1), jnp.where(i == 15, now, 8)))

    @pl.loop(0, MESSAGES + 1)
    def _(i):
        @pl.when(i < MESSAGES)
        def _():
            t_near(i, 0).wait_recv()
            t_next(i, 0).start()
            t_near(i, 1).wait_recv()
            t_next(i, 1).start()

        @pl.when(i + AHEAD < MESSAGES)
        def _():
            t_along_y(i + AHEAD)

        w_step(i + W_LEAD)

        done = i + W_LEAD - 4

        @pl.when((done >= 0) & (done <= 9) & (done % 3 == 0))
        def _():
            for k in range(4):
                w_pair(done // 3, k).wait_recv()

        @pl.when(i >= 1)
        def _():
            t_next(i - 1, 0).wait_recv()
            t_next(i - 1, 1).wait_recv()

        @pl.loop(others_done(i - 1), others_done(i))
        def _(n):
            stage_other(n)

        @pl.loop(owns_done(i - 1), owns_done(i))
        def _(n):
            e = jnp.where(n >= CHUNKS, 1 - early, early)
            stage_own(n % CHUNKS, e)
            stage_u(n % CHUNKS, e)

        @pl.loop(filters_done(i - 1), filters_done(i))
        def _(n):
            stage_filter(n % CHUNKS, jnp.where(n < CHUNKS, early, 1 - early))

    @pl.loop(0, CHUNKS)
    def _(j):
        few = pbuf.at[0, pl.ds(0, 224)]
        some = pbuf.at[0, pl.ds(0, 240)]
        all_ = pbuf.at[0]
        this, that = 2 * j + group(j), 2 * j + 1 - group(j)
        pltpu.make_async_copy(few, few, pr.at[this]).wait()
        pltpu.make_async_copy(all_, all_, pr.at[that]).wait()
        handed[:, at(this, LANES)] = pbuf[this]
        handed[:, at(that, LANES)] = pbuf[that]
        g_copy(j).wait_recv()
        gated[:, at(that, LANES)] = grecv[j]
        g_copy(j).wait_send()
        for e in (0, 1):
            pltpu.make_async_copy(some, some, ps.at[j, e]).wait()
            o_copy(j, e).wait_send()
            h_copy(j, e).wait_send()
        for k in range(4):
            w_pair(j, k).wait_send()

    @pl.loop(0, UNITS)
    def _(v):
        w_beside(v).wait_send()
        w_across(v).wait_send()
        w_far(v).wait_send()

    @pl.loop(0, MESSAGES)
    def _(m):
        for k in (0, 1):
            t_near(m, k).wait_send()
            t_next(m, k).wait_send()

    m_copy().wait_send()
    for sub in range(PARTS):
        t_x(sub).wait_send()
        for d in (0, 1):
            @pl.when(jnp.logical_not(stays(d)))
            def _():
                t_z(0, sub, d).wait_send()
                t_z(1, sub, d).wait_send()


def per_device(tokens, input_weight, filter_taps, decay_rates, skip_gain, owners):
    dma = pltpu.SemaphoreType.DMA
    vmem, any_ = pl.BlockSpec(memory_space=pltpu.VMEM), pl.BlockSpec(memory_space=pl.ANY)
    gated, handed = pl.pallas_call(
        kernel,
        out_shape=(jax.ShapeDtypeStruct((ROWS, 1024), BF16), jax.ShapeDtypeStruct((ROWS, 1024), BF16)),
        in_specs=[any_, any_, vmem, vmem, vmem, vmem],
        out_specs=(vmem, vmem),
        scratch_shapes=[
            pltpu.VMEM((CHUNKS, 8, 3, HALF, LANES), BF16),
            pltpu.VMEM((CHUNKS, 3, HALF, LANES), BF16),
            pltpu.VMEM((4, 2, 2, ROWS, 1024), BF16),
            pltpu.VMEM((ROWS, 1024), BF16),
            pltpu.VMEM((CHUNKS, ROWS, 3 * LANES), F32),
            pltpu.VMEM((CHUNKS, 2, ROWS, 3 * LANES), BF16),
            pltpu.VMEM((CHUNKS, 2, ROWS, 3 * LANES), BF16),
            pltpu.VMEM((CHUNKS, 2, ROWS, LANES), BF16),
            pltpu.VMEM((CHUNKS, 2, ROWS, LANES), BF16),
            pltpu.VMEM((CHUNKS, 2, 128, LANES), BF16),
            pltpu.VMEM((CHUNKS, 2, ROWS, LANES), BF16),
            pltpu.VMEM((2 * CHUNKS, ROWS, LANES), BF16),
            pltpu.VMEM((CHUNKS, ROWS, LANES), BF16),
            pltpu.VMEM((CHUNKS, ROWS, LANES), BF16),
            pltpu.VMEM((32, 128), BF16),
            pltpu.VMEM((32, 128), BF16),
            pltpu.VMEM((2, ROWS, ROWS), BF16),
            pltpu.VMEM((CHUNKS, 128, LANES), F32),
            pltpu.VMEM((8, 376, LANES), F32),
            dma((2, CHUNKS)), dma((7, UNITS)), dma((7, UNITS)),
            dma((PARTS,)), dma((PARTS,)), dma((2, PARTS, 2)), dma((2, 2, PARTS)),
            dma((4, MESSAGES)), dma((4, MESSAGES)),
            dma((CHUNKS, 2)), dma((CHUNKS, 2)), dma((CHUNKS, 2)), dma((CHUNKS, 2)),
            dma((CHUNKS, 2)), dma((2 * CHUNKS,)), dma((CHUNKS,)), dma((CHUNKS,)), dma, dma,
        ],
        compiler_params=pltpu.CompilerParams(
            collective_id=0, has_side_effects=True, vmem_limit_bytes=56 * 1024 * 1024),
        name="hyena",
    )(tokens, input_weight, filter_taps, decay_rates.reshape(1, -1), skip_gain.reshape(1, -1), owners.reshape(1, -1))
    return gated, handed.reshape(32, 8, 1024)


def solution(mesh):
    return jax.shard_map(
        per_device,
        mesh=mesh,
        in_specs=(P("seq", "chan"), P(None, "seq", "chan"), P(None, "chan"), P("chan"), P("chan"), P("seq", None)),
        out_specs=(P("seq", "chan"), P("seq", None, "chan")),
        check_vma=False,
    )
```

```python
import jax
import jax.numpy as jnp
from jax import lax
from jax.experimental import pallas as pl
from jax.experimental.pallas import tpu as pltpu
from jax.sharding import PartitionSpec as P

MESH = pl.DeviceIdType.MESH
F32, BF16 = jnp.float32, jnp.bfloat16
CHUNKS, LANES = 4, 128
ROWS, HALF = 256, 512
PARTS = 4
SUB, MESSAGES = ROWS // PARTS, 4 * PARTS
AHEAD, UNITS, W_AHEAD, W_LEAD = 4, 3 * CHUNKS, 3, 1


def kernel(tok, wgt, taps_in, decay, skip, owners, gated, handed,
           wbuf, wother, tbuf, txbuf, own, osend, orecv, qbuf, ubuf, hrecv, psend, pbuf, gsend, grecv,
           mine, theirs, sel, taps, shifts,
           wl, ws, wr, txs, txr, tzs, tzr, tys, tyr, os_, or_, hs, hr, ps, pr, gs, gr, ms, mr):
    s, c = lax.axis_index("seq"), lax.axis_index("chan")
    core, x, zh = s % 2, (s // 2) % 4, s // 8
    zl, y = c // 4, c % 4
    zo, x2 = 1 - zh, (x + 2) % 4

    def dev(zh_, x_, core_, zl_, y_):
        return ((zh_ * 4 + x_) * 2 + core_, zl_ * 4 + y_)

    def remote(src, dst, ss, rs, to):
        return pltpu.make_async_remote_copy(
            src_ref=src, dst_ref=dst, send_sem=ss, recv_sem=rs, device_id=to, device_id_type=MESH)

    def at(start, size):
        return pl.ds(pl.multiple_of(start * size, size), size)

    def group(j):
        return ((x + j % 2) // 2) % 2

    def beside(j):
        up = 1 - 2 * ((x + j) % 2)
        return (x + 4 + up) % 4

    def across(j):
        up = 1 - 2 * ((x + j + 1) % 2)
        return (x + 4 + up) % 4

    def kb(xx):
        return xx * 2 + core

    def load(j):
        return pltpu.make_async_copy(wgt.at[:, :, at(2 * j + group(j), LANES)], wbuf.at[j, kb(x)], wl.at[0, j])

    def load_other(j):
        return pltpu.make_async_copy(wgt.at[:, :, at(2 * j + 1 - group(j), LANES)], wother.at[j], wl.at[1, j])

    @pl.loop(0, CHUNKS)
    def _(j):
        load(j).start()
        load_other(j).start()

    barrier = pltpu.get_barrier_semaphore()

    partners = [dev(zh, (x + d) % 4, core, zl, y) for d in (1, 2, 3)] + [dev(zh, x, 1 - core, zl, y)]
    partners += [dev(zo, x, core, zl, y), dev(zh, x, core, 1 - zl, y), dev(zo, x, core, 1 - zl, y)]
    partners += [dev(zh, x, core, zl, (y + d) % 4) for d in (1, 3)]
    for partner in partners:
        pl.semaphore_signal(barrier, inc=1, device_id=partner, device_id_type=MESH)
    pl.semaphore_wait(barrier, len(partners))

    def w_beside(v):
        block = wbuf.at[v // 3, kb(x), v % 3]
        return remote(block, block, ws.at[0], wr.at[0, v], dev(zh, beside(v // 3), core, zl, y))

    def w_across(v):
        return remote(wother.at[v // 3, v % 3], wbuf.at[v // 3, kb(x), v % 3], ws.at[0], wr.at[1, v],
                      dev(zh, across(v // 3), core, zl, y))

    def w_far(v):
        block = wbuf.at[v // 3, kb(across(v // 3)), v % 3]
        return remote(block, block, ws.at[0], wr.at[2, v], dev(zh, beside(v // 3), core, zl, y))

    def w_pair(j, k):
        block = wbuf.at[j, kb((x + k) % 4)]
        return remote(block, block, ws.at[1], wr.at[3 + k, j], dev(zh, x, 1 - core, zl, y))

    def w_send(v):
        @pl.when(v % 3 == 0)
        def _():
            load(v // 3).wait()
            load_other(v // 3).wait()

        w_beside(v).start()
        w_across(v).start()

    def w_step(v):
        @pl.when(v < UNITS)
        def _():
            w_across(v).wait_recv()
            w_far(v).start()
            w_beside(v).wait_recv()

            @pl.when(v + W_AHEAD < UNITS)
            def _():
                w_send(v + W_AHEAD)

        @pl.when((v >= 1) & (v <= UNITS))
        def _():
            w_far(v - 1).wait_recv()

            @pl.when(v % 3 == 0)
            def _():
                for k in range(4):
                    w_pair(v // 3 - 1, k).start()

    def t_x(sub):
        return remote(tok.at[at(sub, SUB)], txbuf.at[at(sub, SUB)], txs.at[0], txr.at[sub], dev(zh, x2, core, zl, y))

    def t_z(e, sub, d):
        src = txbuf if e else tok
        return remote(src.at[at(sub, SUB)], tbuf.at[y, zh, e, at(sub, SUB)], tzs.at[e, d], tzr.at[zh, e, sub],
                      dev(zl, x, core, d, y))

    def t_own(e, sub):
        src = txbuf if e else tok
        return pltpu.make_async_copy(src.at[at(sub, SUB)], tbuf.at[y, zh, e, at(sub, SUB)], tzr.at[zh, e, sub])

    def stays(d):
        return jnp.logical_and(zl == zh, zl == d)

    def t_along_z(e, sub):
        for d in (0, 1):
            @pl.when(stays(d))
            def _():
                t_own(e, sub).start()

            @pl.when(jnp.logical_not(stays(d)))
            def _():
                t_z(e, sub, d).start()

    early = x // 2

    def block_of(m):
        r = m // PARTS
        return jnp.where(r < 2, zo, zh), jnp.where(r < 2, r, (early + r) % 2)

    def t_piece(yy, m):
        z, e = block_of(m)
        return tbuf.at[yy, z, e, at(m % PARTS, SUB)]

    def t_near(m, k):
        piece = t_piece(y, m)
        return remote(piece, piece, tys.at[0], tyr.at[k, m], dev(zh, x, core, zl, (y + 1 + 2 * k) % 4))

    def t_next(m, k):
        z, e = block_of(m)
        piece = tbuf.at[(y + 3 - 2 * k) % 4, z, e, at((m % PARTS) * 2 + k, SUB // 2)]
        return remote(piece, piece, tys.at[0], tyr.at[2 + k, m], dev(zh, x, core, zl, (y + 1 + 2 * k) % 4))

    def t_along_y(m):
        z, e = block_of(m)
        piece = t_piece(y, m)
        pltpu.make_async_copy(piece, piece, tzr.at[z, e, m % PARTS]).wait()
        t_near(m, 0).start()
        t_near(m, 1).start()

    for sub in range(PARTS):
        t_x(sub).start()
    for sub in range(PARTS):
        t_along_z(0, sub)
    for v in range(W_AHEAD):
        w_send(v)

    iota = lambda shape, axis: lax.broadcasted_iota(jnp.int32, shape, axis)
    dot = lambda a, b, dims: lax.dot_general(a, b, (dims, ((), ())), preferred_element_type=F32)
    onehot = (jnp.broadcast_to(owners[...], (32, 32)) == iota((32, 32), 0)).astype(F32)
    before = (iota((32, 32), 0) < iota((32, 32), 1)).astype(BF16)
    earlier = dot(onehot.astype(BF16), before, ((1,), (0,)))
    target = owners[...].astype(F32) * 2.0 + jnp.sum(earlier * onehot, axis=0, keepdims=True)
    place = (jnp.broadcast_to(target, (32, 32)) == iota((32, 32), 0).astype(F32)).astype(F32)
    mine[...] = jnp.concatenate([place, jnp.zeros((32, 96), F32)], axis=1).astype(BF16)

    def m_copy():
        return remote(mine, theirs, ms, mr, dev(zh, x2, core, zl, y))

    m_copy().start()
    t_along_y(0)
    t_along_y(1)
    w_step(0)
    for sub in range(PARTS):
        t_x(sub).wait_recv()
        t_along_z(1, sub)
        if sub + 2 < AHEAD:
            t_along_y(sub + 2)
        if sub + 1 < W_LEAD:
            w_step(sub + 1)

    def order(place):
        spread = (iota((ROWS, 32), 0) // 8 == iota((ROWS, 32), 1)).astype(BF16)
        part = dot(spread, place[:, :32], ((1,), (0,))).astype(BF16)
        whole = dot(part, spread, ((1,), (1,)))
        same = (iota((ROWS, ROWS), 0) % 8 == iota((ROWS, ROWS), 1) % 8).astype(F32)
        return (whole * same).astype(BF16)

    sel[0] = order(mine[...])
    m_copy().wait_recv()
    sel[1] = order(theirs[...])

    lag = iota((128, LANES), 0)

    @pl.loop(0, CHUNKS)
    def _(j):
        cols = at(2 * j + group(j), LANES)
        value = taps_in[:, cols] * jnp.exp(-decay[:, cols] * lag.astype(F32))
        taps[j] = value + jnp.where(lag == 0, skip[:, cols], 0.0)

    def matmul(j, z, e):
        t = jnp.concatenate([tbuf[yy, z, e] for yy in range(4)], axis=1)
        w = jnp.concatenate([jnp.concatenate([wbuf[j, k, p] for k in range(8)], axis=0) for p in range(3)], axis=1)
        return jnp.dot(t, w, preferred_element_type=F32)

    def o_copy(j, e):
        return remote(osend.at[j, e], orecv.at[j, e], os_.at[0], or_.at[j, e], dev(zo, x, core, zl, y))

    def h_copy(j, e):
        xe = (x + 2 * e) % 4
        to = beside(j)
        same = jnp.where((xe + 1) % 4 == to, 0, 1)
        to_x, to_zh = jnp.where(core == 0, x, to), jnp.where(core == 0, zh, (zh + xe // 3) % 2)
        to_e = jnp.where(core == 0, e, same)
        return remote(ubuf.at[j, e, pl.ds(128, 128)], hrecv.at[j, to_e], hs.at[0], hr.at[j, to_e],
                      dev(to_zh, to_x, 1 - core, zl, y))

    def p_copy(e, o):
        to, source = (s + o) % 16, (zh * 4 + (x + 2 * e) % 4) * 2 + core
        return remote(psend.at[e, :, at(to, 16)], pbuf.at[e, :, at(source, 16)], ps.at[e], pr.at[e], (to, c))

    def stage_pages(e):
        @pl.loop(1, 16)
        def _(o):
            p_copy(e, o).start()

        source = (zh * 4 + (x + 2 * e) % 4) * 2 + core
        pbuf[e, :, at(source, 16)] = psend[e, :, at(s, 16)]

    def g_copy(j):
        return remote(gsend.at[j], grecv.at[j], gs.at[0], gr.at[j], dev(zh, x2, core, zl, y))

    def stage_other(n):
        e = jnp.where(n < 2, 0, jnp.where(n < 4, 1, n % 2))
        j = jnp.where(n < 2, n, jnp.where(n < 4, n - 2, n // 2))
        osend[j, e] = matmul(j, zo, e).astype(BF16)
        o_copy(j, e).start()

    def stage_own(n):
        late = n // 4
        pair = jnp.where(n < 4, n // 2, n % 2)
        rows = at(jnp.where(n < 4, n % 2, (n - 4) // 2), ROWS // 2)
        e = jnp.where(n < 4, early, 1 - early)
        t = jnp.concatenate([tbuf[yy, zh, e, rows] for yy in range(4)], axis=1)
        w = jnp.concatenate([jnp.concatenate([wbuf[2 * pair + q, k, p] for k in range(8)], axis=0)
                             for q in (0, 1) for p in range(3)], axis=1)
        both = jnp.dot(t, w, preferred_element_type=F32)
        for q in (0, 1):
            own[late, 2 * pair + q, rows] = both[:, 3 * LANES * q:3 * LANES * (q + 1)]

    def stage_u(j, e, late):
        o_copy(j, e).wait_recv()
        full = (own[late, j] + orecv[j, e].astype(F32)).astype(BF16)
        qbuf[j, e] = full[:, :LANES]
        u = (full[:, LANES:2 * LANES].astype(F32) * full[:, 2 * LANES:].astype(F32)).astype(BF16)
        ubuf[j, e] = u
        h_copy(j, e).start()
        psend[e, j] = jnp.dot(sel[e], u, preferred_element_type=F32).astype(BF16)

        @pl.when(j == CHUNKS - 1)
        def _():
            stage_pages(e)

    def stage_filter(j, e):
        pltpu.make_async_copy(hrecv.at[j, e], hrecv.at[j, e], hr.at[j, e]).wait()
        first = (zh == 0) & (core == 0) & ((x + 2 * e) % 4 == 0)
        prior = jnp.where(first, 0.0, hrecv[j, e].astype(F32))
        ext = jnp.concatenate([prior, ubuf[j, e].astype(F32)], axis=0)
        for b in range(8):
            shifts[b] = ext[8 - b:384 - b]

        def stream(count, tap, data):
            def add(b, sums):
                x_ = [data(b, m) for m in range(count + 7)]
                sums = list(sums)
                for a in range(8):
                    weight = jnp.broadcast_to(tap(b, a), (8, LANES))
                    for r in range(count):
                        sums[r] = sums[r] + weight * x_[r - a + 7]
                return tuple(sums)
            return lax.fori_loop(0, 8, add, tuple(jnp.zeros((8, LANES), F32) for _ in range(count)), unroll=2)

        def rows_of(b, m):
            return shifts[b, 8 * m:8 * m + 8]

        def tap_of(b, a):
            return taps[j, pl.ds(8 * a + b, 1)]

        even = stream(16, lambda b, a: tap_of(b, 2 * a), lambda b, m: rows_of(b, 2 * m + 1))
        odd = stream(17, lambda b, a: tap_of(b, 2 * a + 1), lambda b, m: rows_of(b, 2 * m))
        both = stream(16, lambda b, a: tap_of(b, 2 * a) + tap_of(b, 2 * a + 1),
                      lambda b, m: rows_of(b, 2 * m + 1) + rows_of(b, 2 * m + 2))
        z = jnp.concatenate(
            [piece for r in range(16) for piece in (even[r] + odd[r], both[r] - even[r] - odd[r + 1])], axis=0)
        out = (qbuf[j, e].astype(F32) * z).astype(BF16)

        @pl.when(e == 1)
        def _():
            gsend[j] = out
            g_copy(j).start()

        @pl.when(e == 0)
        def _():
            gated[:, at(2 * j + group(j), LANES)] = out

    waits = (zh == 1) & (core == 0) & (x % 2 == 0)
    now = jnp.where(waits, 0, 3)

    def others_done(i):
        return jnp.where(i < 4, 0, jnp.where(i < 8, i // 2 - 1, jnp.where(i < 11, i - 4, jnp.where(i < 12, 6, 8))))

    def owns_done(i):
        return jnp.where(i < 13, 0, jnp.where(i < 16, 2 * (i - 12), 6))

    def us_done(i):
        return jnp.where(i < 13, 0, jnp.where(i == 13, 2, jnp.where(i < 16, 3, 8)))

    def filters_done(i):
        return jnp.where(i < 16, 0, 8)

    @pl.loop(0, MESSAGES + 1)
    def _(i):
        @pl.when(i < MESSAGES)
        def _():
            t_near(i, 0).wait_recv()
            t_next(i, 0).start()
            t_near(i, 1).wait_recv()
            t_next(i, 1).start()

        @pl.when(i + AHEAD < MESSAGES)
        def _():
            t_along_y(i + AHEAD)

        w_step(i + W_LEAD)

        done = i + W_LEAD - 4

        @pl.when((done >= 0) & (done <= 9) & (done % 3 == 0))
        def _():
            for k in range(4):
                w_pair(done // 3, k).wait_recv()

        @pl.when(i >= 1)
        def _():
            t_next(i - 1, 0).wait_recv()
            t_next(i - 1, 1).wait_recv()

        @pl.loop(others_done(i - 1), others_done(i))
        def _(n):
            stage_other(n)

        @pl.loop(owns_done(i - 1), owns_done(i))
        def _(n):
            stage_own(n)

        @pl.loop(us_done(i - 1), us_done(i))
        def _(n):
            late = n // CHUNKS

            @pl.when((late == 1) & (n % 2 == 0))
            def _():
                stage_own(6 + n % CHUNKS // 2)

            stage_u(n % CHUNKS, jnp.where(late == 1, 1 - early, early), late)

        @pl.loop(filters_done(i - 1), filters_done(i))
        def _(n):
            stage_filter(n % CHUNKS, jnp.where(n < CHUNKS, early, 1 - early))

    def sent(ref, sem):
        pltpu.make_async_copy(ref, ref, sem).wait()

    sent(tbuf.at[pl.ds(0, 3)], tys.at[0])
    sent(wbuf.at[pl.ds(0, 2), pl.ds(0, 6)], ws.at[0])
    sent(wbuf.at[pl.ds(0, 2)], ws.at[1])
    sent(osend, os_.at[0])
    sent(hrecv, hs.at[0])
    sent(mine, ms)
    sent(txbuf, txs.at[0])
    for e in (0, 1):
        for d in (0, 1):
            @pl.when(jnp.logical_not(stays(d)))
            def _():
                sent(txbuf, tzs.at[e, d])

    for e in (0, 1):
        sent(pbuf.at[e, :, pl.ds(0, 240)], ps.at[e])
        sent(pbuf.at[e, :, pl.ds(0, 240)], pr.at[e])

    @pl.loop(0, 16)
    def _(source):
        rows = at(source, 16)
        for e in (0, 1):
            there = (source // 2 + 2 * e) % 4
            for j in range(CHUNKS):
                handed[rows, at(2 * j + ((there + j % 2) // 2) % 2, LANES)] = pbuf[e, j, rows]

    for j in range(CHUNKS):
        g_copy(j).wait_recv()
        gated[:, at(2 * j + 1 - group(j), LANES)] = grecv[j]
    sent(gsend, gs.at[0])


def per_device(tokens, input_weight, filter_taps, decay_rates, skip_gain, owners):
    dma = pltpu.SemaphoreType.DMA
    vmem, any_ = pl.BlockSpec(memory_space=pltpu.VMEM), pl.BlockSpec(memory_space=pl.ANY)
    gated, handed = pl.pallas_call(
        kernel,
        out_shape=(jax.ShapeDtypeStruct((ROWS, 1024), BF16), jax.ShapeDtypeStruct((ROWS, 1024), BF16)),
        in_specs=[any_, any_, vmem, vmem, vmem, vmem],
        out_specs=(vmem, vmem),
        scratch_shapes=[
            pltpu.VMEM((CHUNKS, 8, 3, HALF, LANES), BF16),
            pltpu.VMEM((CHUNKS, 3, HALF, LANES), BF16),
            pltpu.VMEM((4, 2, 2, ROWS, 1024), BF16),
            pltpu.VMEM((ROWS, 1024), BF16),
            pltpu.VMEM((2, CHUNKS, ROWS, 3 * LANES), F32),
            pltpu.VMEM((CHUNKS, 2, ROWS, 3 * LANES), BF16),
            pltpu.VMEM((CHUNKS, 2, ROWS, 3 * LANES), BF16),
            pltpu.VMEM((CHUNKS, 2, ROWS, LANES), BF16),
            pltpu.VMEM((CHUNKS, 2, ROWS, LANES), BF16),
            pltpu.VMEM((CHUNKS, 2, 128, LANES), BF16),
            pltpu.VMEM((2, CHUNKS, ROWS, LANES), BF16),
            pltpu.VMEM((2, CHUNKS, ROWS, LANES), BF16),
            pltpu.VMEM((CHUNKS, ROWS, LANES), BF16),
            pltpu.VMEM((CHUNKS, ROWS, LANES), BF16),
            pltpu.VMEM((32, 128), BF16),
            pltpu.VMEM((32, 128), BF16),
            pltpu.VMEM((2, ROWS, ROWS), BF16),
            pltpu.VMEM((CHUNKS, 128, LANES), F32),
            pltpu.VMEM((8, 376, LANES), F32),
            dma((2, CHUNKS)), dma((2,)), dma((7, UNITS)),
            dma((1,)), dma((PARTS,)), dma((2, 2)), dma((2, 2, PARTS)),
            dma((1,)), dma((4, MESSAGES)),
            dma((1,)), dma((CHUNKS, 2)), dma((1,)), dma((CHUNKS, 2)),
            dma((2,)), dma((2,)), dma((1,)), dma((CHUNKS,)), dma, dma,
        ],
        compiler_params=pltpu.CompilerParams(
            collective_id=0, has_side_effects=True, vmem_limit_bytes=56 * 1024 * 1024),
        name="hyena",
    )(tokens, input_weight, filter_taps, decay_rates.reshape(1, -1), skip_gain.reshape(1, -1), owners.reshape(1, -1))
    def place(a, b, a_out, b_out):
        a_out[...] = a[...]
        b_out[...] = b[...]

    gated, handed = pl.pallas_call(
        place, out_shape=(jax.ShapeDtypeStruct((ROWS, 1024), BF16),) * 2, in_specs=[vmem, vmem], out_specs=(vmem, vmem),
        name="results",
    )(gated, handed)
    return gated, handed.reshape(32, 8, 1024)


def solution(mesh):
    return jax.shard_map(
        per_device,
        mesh=mesh,
        in_specs=(P("seq", "chan"), P(None, "seq", "chan"), P(None, "chan"), P("chan"), P("chan"), P("seq", None)),
        out_specs=(P("seq", "chan"), P("seq", None, "chan")),
        check_vma=False,
    )
```

```python
import jax
import jax.numpy as jnp
from jax import lax
from jax.experimental import pallas as pl
from jax.experimental.pallas import tpu as pltpu
from jax.sharding import PartitionSpec as P

MESH = pl.DeviceIdType.MESH
F32, BF16 = jnp.float32, jnp.bfloat16
CHUNKS, LANES = 4, 128
ROWS, HALF = 256, 512
PARTS = 4
SUB, MESSAGES = ROWS // PARTS, 4 * PARTS
ORDER = [(m + PARTS // 2) % PARTS for m in range(PARTS)]
HALF_ROWS = ROWS // 2
AHEAD, UNITS, W_AHEAD, W_LEAD = 5, 3 * CHUNKS, 3, 1


def kernel(tok, wgt, taps_in, decay, skip, owners, gated, handed,
           wbuf, wother, tbuf, txbuf, own, osend, orecv, qbuf, ubuf, hrecv, psend, pbuf, gsend, grecv,
           mine, theirs, sel, taps, shifts, prior,
           wl, ws, wr, txs, txr, tzs, tzr, tys, tyr, os_, or_, hs, hr, ps, pr, gs, gr, ms, mr):
    s, c = lax.axis_index("seq"), lax.axis_index("chan")
    core, x, zh = s % 2, (s // 2) % 4, s // 8
    zl, y = c // 4, c % 4
    zo, x2 = 1 - zh, (x + 2) % 4

    def dev(zh_, x_, core_, zl_, y_):
        return ((zh_ * 4 + x_) * 2 + core_, zl_ * 4 + y_)

    def remote(src, dst, ss, rs, to):
        return pltpu.make_async_remote_copy(
            src_ref=src, dst_ref=dst, send_sem=ss, recv_sem=rs, device_id=to, device_id_type=MESH)

    def at(start, size):
        return pl.ds(pl.multiple_of(start * size, size), size)

    def group(j):
        return ((x + j % 2) // 2) % 2

    def beside(j):
        up = 1 - 2 * ((x + j) % 2)
        return (x + 4 + up) % 4

    def across(j):
        up = 1 - 2 * ((x + j + 1) % 2)
        return (x + 4 + up) % 4

    def kb(xx):
        return xx * 2 + core

    def load(j):
        return pltpu.make_async_copy(wgt.at[:, :, at(2 * j + group(j), LANES)], wbuf.at[j, kb(x)], wl.at[0, j])

    def load_other(j):
        return pltpu.make_async_copy(wgt.at[:, :, at(2 * j + 1 - group(j), LANES)], wother.at[j], wl.at[1, j])

    @pl.loop(0, CHUNKS)
    def _(j):
        load(j).start()
        load_other(j).start()

    barrier = pltpu.get_barrier_semaphore()

    partners = [dev(zh, (x + d) % 4, core, zl, y) for d in (1, 2, 3)] + [dev(zh, x, 1 - core, zl, y)]
    partners += [dev(zo, x, core, zl, y), dev(zh, x, core, 1 - zl, y), dev(zo, x, core, 1 - zl, y)]
    partners += [dev(zh, x, core, zl, (y + d) % 4) for d in (1, 3)]
    for partner in partners:
        pl.semaphore_signal(barrier, inc=1, device_id=partner, device_id_type=MESH)
    pl.semaphore_wait(barrier, len(partners))

    def w_beside(v):
        block = wbuf.at[v // 3, kb(x), v % 3]
        return remote(block, block, ws.at[0], wr.at[0, v], dev(zh, beside(v // 3), core, zl, y))

    def w_across(v):
        return remote(wother.at[v // 3, v % 3], wbuf.at[v // 3, kb(x), v % 3], ws.at[0], wr.at[1, v],
                      dev(zh, across(v // 3), core, zl, y))

    def w_far(v):
        block = wbuf.at[v // 3, kb(across(v // 3)), v % 3]
        return remote(block, block, ws.at[0], wr.at[2, v], dev(zh, beside(v // 3), core, zl, y))

    def w_pair(j, k):
        block = wbuf.at[j, kb((x + k) % 4)]
        return remote(block, block, ws.at[1], wr.at[3 + k, j], dev(zh, x, 1 - core, zl, y))

    def w_send(v):
        @pl.when(v % 3 == 0)
        def _():
            load(v // 3).wait()
            load_other(v // 3).wait()

        w_beside(v).start()
        w_across(v).start()

    def w_step(v):
        @pl.when(v < UNITS)
        def _():
            w_across(v).wait_recv()
            w_far(v).start()
            w_beside(v).wait_recv()

            @pl.when(v + W_AHEAD < UNITS)
            def _():
                w_send(v + W_AHEAD)

        @pl.when((v >= 1) & (v <= UNITS))
        def _():
            w_far(v - 1).wait_recv()

            @pl.when(v % 3 == 0)
            def _():
                for k in range(4):
                    w_pair(v // 3 - 1, k).start()

    def t_x(sub):
        return remote(tok.at[at(sub, SUB)], txbuf.at[at(sub, SUB)], txs.at[0], txr.at[sub], dev(zh, x2, core, zl, y))

    def t_z(e, sub, d):
        src = txbuf if e else tok
        return remote(src.at[at(sub, SUB)], tbuf.at[y, zh, e, at(sub, SUB)], tzs.at[e, d], tzr.at[zh, e, sub],
                      dev(zl, x, core, d, y))

    def t_own(e, sub):
        src = txbuf if e else tok
        return pltpu.make_async_copy(src.at[at(sub, SUB)], tbuf.at[y, zh, e, at(sub, SUB)], tzr.at[zh, e, sub])

    def stays(d):
        return jnp.logical_and(zl == zh, zl == d)

    def t_along_z(e, sub):
        for d in (0, 1):
            @pl.when(stays(d))
            def _():
                t_own(e, sub).start()

            @pl.when(jnp.logical_not(stays(d)))
            def _():
                t_z(e, sub, d).start()

    early = x // 2

    def block_of(m):
        r = m // PARTS
        return jnp.where(r < 2, zo, zh), jnp.where(r < 2, r, (early + r) % 2)

    def part_of(m):
        return (m + PARTS // 2) % PARTS

    def t_piece(yy, m):
        z, e = block_of(m)
        return tbuf.at[yy, z, e, at(part_of(m), SUB)]

    def t_near(m, k):
        piece = t_piece(y, m)
        return remote(piece, piece, tys.at[0], tyr.at[k, m], dev(zh, x, core, zl, (y + 1 + 2 * k) % 4))

    def t_next(m, k):
        z, e = block_of(m)
        piece = tbuf.at[(y + 3 - 2 * k) % 4, z, e, at(part_of(m) * 2 + k, SUB // 2)]
        return remote(piece, piece, tys.at[0], tyr.at[2 + k, m], dev(zh, x, core, zl, (y + 1 + 2 * k) % 4))

    def t_along_y(m):
        z, e = block_of(m)
        piece = t_piece(y, m)
        pltpu.make_async_copy(piece, piece, tzr.at[z, e, part_of(m)]).wait()
        t_near(m, 0).start()
        t_near(m, 1).start()

    for sub in ORDER:
        t_x(sub).start()
        t_along_z(0, sub)
    for v in range(W_AHEAD):
        w_send(v)

    iota = lambda shape, axis: lax.broadcasted_iota(jnp.int32, shape, axis)
    dot = lambda a, b, dims: lax.dot_general(a, b, (dims, ((), ())), preferred_element_type=F32)
    onehot = (jnp.broadcast_to(owners[...], (32, 32)) == iota((32, 32), 0)).astype(F32)
    before = (iota((32, 32), 0) < iota((32, 32), 1)).astype(BF16)
    earlier = dot(onehot.astype(BF16), before, ((1,), (0,)))
    target = owners[...].astype(F32) * 2.0 + jnp.sum(earlier * onehot, axis=0, keepdims=True)
    place = (jnp.broadcast_to(target, (32, 32)) == iota((32, 32), 0).astype(F32)).astype(F32)
    mine[...] = jnp.concatenate([place, jnp.zeros((32, 96), F32)], axis=1).astype(BF16)

    def m_copy():
        return remote(mine, theirs, ms, mr, dev(zh, x2, core, zl, y))

    m_copy().start()
    t_along_y(0)
    t_along_y(1)
    w_step(0)
    for step, sub in enumerate(ORDER):
        t_x(sub).wait_recv()
        t_along_z(1, sub)
        if step + 2 < AHEAD:
            t_along_y(step + 2)
        if step + 1 < W_LEAD:
            w_step(step + 1)

    def order(place):
        spread = (iota((ROWS, 32), 0) // 8 == iota((ROWS, 32), 1)).astype(BF16)
        part = dot(spread, place[:, :32], ((1,), (0,))).astype(BF16)
        whole = dot(part, spread, ((1,), (1,)))
        same = (iota((ROWS, ROWS), 0) % 8 == iota((ROWS, ROWS), 1) % 8).astype(F32)
        return (whole * same).astype(BF16)

    sel[0] = order(mine[...])
    m_copy().wait_recv()
    sel[1] = order(theirs[...])

    lag = iota((128, LANES), 0)

    @pl.loop(0, CHUNKS)
    def _(j):
        cols = at(2 * j + group(j), LANES)
        value = taps_in[:, cols] * jnp.exp(-decay[:, cols] * lag.astype(F32))
        taps[j] = value + jnp.where(lag == 0, skip[:, cols], 0.0)

    def matmul(j, z, e):
        t = jnp.concatenate([tbuf[yy, z, e] for yy in range(4)], axis=1)
        w = jnp.concatenate([jnp.concatenate([wbuf[j, k, p] for k in range(8)], axis=0) for p in range(3)], axis=1)
        return jnp.dot(t, w, preferred_element_type=F32)

    def o_copy(j, e):
        return remote(osend.at[j, e], orecv.at[j, e], os_.at[0], or_.at[j, e], dev(zo, x, core, zl, y))

    def h_copy(j, e):
        xe = (x + 2 * e) % 4
        to = beside(j)
        same = jnp.where((xe + 1) % 4 == to, 0, 1)
        to_x, to_zh = jnp.where(core == 0, x, to), jnp.where(core == 0, zh, (zh + xe // 3) % 2)
        to_e = jnp.where(core == 0, e, same)
        return remote(ubuf.at[j, e, pl.ds(128, 128)], hrecv.at[j, to_e], hs.at[0], hr.at[j, to_e],
                      dev(to_zh, to_x, 1 - core, zl, y))

    def p_copy(e, o):
        to, source = (s + o) % 16, (zh * 4 + (x + 2 * e) % 4) * 2 + core
        return remote(psend.at[e, :, at(to, 16)], pbuf.at[e, :, at(source, 16)], ps.at[e], pr.at[e], (to, c))

    def stage_pages(e):
        @pl.loop(1, 16)
        def _(o):
            p_copy(e, o).start()

        source = (zh * 4 + (x + 2 * e) % 4) * 2 + core
        pbuf[e, :, at(source, 16)] = psend[e, :, at(s, 16)]

    def g_copy(j, rows):
        return remote(gsend.at[j, rows], grecv.at[j, rows], gs.at[0], gr.at[0], dev(zh, x2, core, zl, y))

    def matmul_pair(pair, z, e, rows):
        t = jnp.concatenate([tbuf[yy, z, e, rows] for yy in range(4)], axis=1)
        w = jnp.concatenate([jnp.concatenate([wbuf[2 * pair + q, k, p] for k in range(8)], axis=0)
                             for q in (0, 1) for p in range(3)], axis=1)
        both = jnp.dot(t, w, preferred_element_type=F32)
        return both[:, :3 * LANES], both[:, 3 * LANES:]

    def stage_other(n):
        e = jnp.where(n < 2, 0, jnp.where(n % 2 == 0, early, 1 - early))
        j = jnp.where(n < 2, n, n // 2 + 1)
        osend[j, e] = matmul(j, zo, e).astype(BF16)
        o_copy(j, e).start()

    def stage_other_half(half):
        rows = at(half, HALF_ROWS)
        for j, part in enumerate(matmul_pair(0, zo, 1, rows)):
            osend[j, 1, rows] = part.astype(BF16)
            remote(osend.at[j, 1, rows], orecv.at[j, 1, rows], os_.at[0], or_.at[j, 1], dev(zo, x, core, zl, y)).start()

    def stage_own(n):
        late = n // 4
        pair = jnp.where(n < 4, n // 2, n % 2)
        rows = at(jnp.where(n < 4, n % 2, 1 - (n - 4) // 2), HALF_ROWS)
        e = jnp.where(n < 4, early, 1 - early)
        for q, part in enumerate(matmul_pair(pair, zh, e, rows)):
            own[late, 2 * pair + q, rows] = part

    def stage_u(n):
        late = n // 8
        j = jnp.where(n < 8, n // 2, n % 4)
        half = 1 - jnp.where(n < 8, n % 2, (n - 8) // 4)
        e, rows = jnp.where(n < 8, early, 1 - early), at(half, HALF_ROWS)

        @pl.when(half == 1)
        def _():
            o_copy(j, e).wait_recv()

        full = (own[late, j, rows] + orecv[j, e, rows].astype(F32)).astype(BF16)
        qbuf[j, e, rows] = full[:, :LANES]
        ubuf[j, e, rows] = (full[:, LANES:2 * LANES].astype(F32) * full[:, 2 * LANES:].astype(F32)).astype(BF16)

        @pl.when(half == 1)
        def _():
            h_copy(j, e).start()

        @pl.when((n == 7) | (n == 15))
        def _():
            @pl.loop(0, CHUNKS)
            def _(jj):
                psend[e, jj] = jnp.dot(sel[e], ubuf[jj, e], preferred_element_type=F32).astype(BF16)

            stage_pages(e)

    def wait_prior(j, e):
        pltpu.make_async_copy(hrecv.at[j, e], hrecv.at[j, e], hr.at[j, e]).wait()
        first = (zh == 0) & (core == 0) & ((x + 2 * e) % 4 == 0)
        return jnp.where(first, 0.0, hrecv[j, e].astype(F32))

    def filtered(j, before, u):
        count = u.shape[0] // 16
        ext = jnp.concatenate([before, u.astype(F32)], axis=0)
        for b in range(8):
            shifts[b, :ext.shape[0] - 8] = ext[8 - b:ext.shape[0] - b]

        def stream(groups, tap, data):
            sums = [jnp.zeros((8, LANES), F32) for _ in range(groups)]
            for b in range(8):
                x_ = [data(b, m) for m in range(groups + 7)]
                for a in range(8):
                    weight = jnp.broadcast_to(tap(b, a), (8, LANES))
                    for r in range(groups):
                        sums[r] = sums[r] + weight * x_[r - a + 7]
            return sums

        def rows_of(b, m):
            return shifts[b, 8 * m:8 * m + 8]

        def tap_of(b, a):
            return taps[j, 8 * a + b:8 * a + b + 1]

        even = stream(count, lambda b, a: tap_of(b, 2 * a), lambda b, m: rows_of(b, 2 * m + 1))
        odd = stream(count + 1, lambda b, a: tap_of(b, 2 * a + 1), lambda b, m: rows_of(b, 2 * m))
        both = stream(count, lambda b, a: tap_of(b, 2 * a) + tap_of(b, 2 * a + 1),
                      lambda b, m: rows_of(b, 2 * m + 1) + rows_of(b, 2 * m + 2))
        return jnp.concatenate(
            [piece for r in range(count) for piece in (even[r] + odd[r], both[r] - even[r] - odd[r + 1])], axis=0)

    def finish(j, e, rows, z):
        out = (qbuf[j, e, rows].astype(F32) * z).astype(BF16)

        @pl.when(e == 1)
        def _():
            gsend[j, rows] = out
            g_copy(j, rows).start()

        @pl.when(e == 0)
        def _():
            gated[rows, at(2 * j + group(j), LANES)] = out

    def stage_filter(j, half):
        @pl.when(half == 0)
        def _():
            prior[...] = wait_prior(j, early)

        @pl.when(half == 1)
        def _():
            prior[...] = ubuf[j, early, :HALF_ROWS].astype(F32)

        rows = at(half, HALF_ROWS)
        finish(j, early, rows, filtered(j, prior[...], ubuf[j, early, rows]))

    def stage_filter_whole(j):
        e = 1 - early
        finish(j, e, pl.ds(0, ROWS), filtered(j, wait_prior(j, e), ubuf[j, e]))

    def others_done(i):
        return jnp.where(i < 4, 0, jnp.where(i < 9, jnp.minimum(i // 2 - 1, 2), jnp.where(i < 12, 4, 6)))

    def owns_done(i):
        return jnp.where(i < 13, 0, jnp.where(i < 16, 2 * (i - 12), 6))

    def us_done(i):
        return jnp.where(i < 13, 0, jnp.where(i == 13, 4, jnp.where(i == 14, 6, jnp.where(i == 15, 12, 16))))

    def filters_done(i):
        return jnp.where(i < 14, 0, jnp.where(i == 14, 2, jnp.where(i == 15, 4, 12)))

    @pl.loop(0, MESSAGES + 1)
    def _(i):
        @pl.when(i < MESSAGES)
        def _():
            t_near(i, 0).wait_recv()
            t_next(i, 0).start()
            t_near(i, 1).wait_recv()
            t_next(i, 1).start()

        @pl.when(i + AHEAD < MESSAGES)
        def _():
            t_along_y(i + AHEAD)

        w_step(i + W_LEAD)

        done = i + W_LEAD - 4

        @pl.when((done >= 0) & (done <= 9) & (done % 3 == 0))
        def _():
            for k in range(4):
                w_pair(done // 3, k).wait_recv()

        @pl.when(i >= 1)
        def _():
            t_next(i - 1, 0).wait_recv()
            t_next(i - 1, 1).wait_recv()

        @pl.loop(others_done(i - 1), others_done(i))
        def _(n):
            stage_other(n)

        @pl.when((i == 6) | (i == 8))
        def _():
            stage_other_half((8 - i) // 2)

        @pl.loop(owns_done(i - 1), owns_done(i))
        def _(n):
            stage_own(n)

        @pl.loop(us_done(i - 1), us_done(i))
        def _(n):
            @pl.when((n == 12) | (n == 14))
            def _():
                stage_own(n // 2)

            stage_u(n)

        @pl.loop(filters_done(i - 1), filters_done(i))
        def _(n):
            sooner = (n < 4) | ((n // 4 + early) % 2 == 0)

            @pl.when(sooner)
            def _():
                stage_filter(n % 4, jnp.where(n < 4, 1, 0))

            @pl.when(jnp.logical_not(sooner))
            def _():
                stage_filter_whole(n % 4)

    def sent(ref, sem):
        pltpu.make_async_copy(ref, ref, sem).wait()

    sent(tbuf.at[pl.ds(0, 3)], tys.at[0])
    sent(wbuf.at[pl.ds(0, 2), pl.ds(0, 6)], ws.at[0])
    sent(wbuf.at[pl.ds(0, 2)], ws.at[1])
    sent(osend, os_.at[0])
    sent(hrecv, hs.at[0])
    sent(mine, ms)
    sent(txbuf, txs.at[0])
    for e in (0, 1):
        for d in (0, 1):
            @pl.when(jnp.logical_not(stays(d)))
            def _():
                sent(txbuf, tzs.at[e, d])

    for e in (0, 1):
        sent(pbuf.at[e, :, pl.ds(0, 240)], ps.at[e])
        sent(pbuf.at[e, :, pl.ds(0, 240)], pr.at[e])

    @pl.loop(0, 16)
    def _(source):
        rows = at(source, 16)
        for e in (0, 1):
            there = (source // 2 + 2 * e) % 4
            for j in range(CHUNKS):
                handed[rows, at(2 * j + ((there + j % 2) // 2) % 2, LANES)] = pbuf[e, j, rows]

    sent(gsend, gr.at[0])
    for j in range(CHUNKS):
        gated[:, at(2 * j + 1 - group(j), LANES)] = grecv[j]
    sent(gsend, gs.at[0])


def per_device(tokens, input_weight, filter_taps, decay_rates, skip_gain, owners):
    dma = pltpu.SemaphoreType.DMA
    vmem, any_ = pl.BlockSpec(memory_space=pltpu.VMEM), pl.BlockSpec(memory_space=pl.ANY)
    gated, handed = pl.pallas_call(
        kernel,
        out_shape=(jax.ShapeDtypeStruct((ROWS, 1024), BF16), jax.ShapeDtypeStruct((ROWS, 1024), BF16)),
        in_specs=[any_, any_, vmem, vmem, vmem, vmem],
        out_specs=(vmem, vmem),
        scratch_shapes=[
            pltpu.VMEM((CHUNKS, 8, 3, HALF, LANES), BF16),
            pltpu.VMEM((CHUNKS, 3, HALF, LANES), BF16),
            pltpu.VMEM((4, 2, 2, ROWS, 1024), BF16),
            pltpu.VMEM((ROWS, 1024), BF16),
            pltpu.VMEM((2, CHUNKS, ROWS, 3 * LANES), F32),
            pltpu.VMEM((CHUNKS, 2, ROWS, 3 * LANES), BF16),
            pltpu.VMEM((CHUNKS, 2, ROWS, 3 * LANES), BF16),
            pltpu.VMEM((CHUNKS, 2, ROWS, LANES), BF16),
            pltpu.VMEM((CHUNKS, 2, ROWS, LANES), BF16),
            pltpu.VMEM((CHUNKS, 2, 128, LANES), BF16),
            pltpu.VMEM((2, CHUNKS, ROWS, LANES), BF16),
            pltpu.VMEM((2, CHUNKS, ROWS, LANES), BF16),
            pltpu.VMEM((CHUNKS, ROWS, LANES), BF16),
            pltpu.VMEM((CHUNKS, ROWS, LANES), BF16),
            pltpu.VMEM((32, 128), BF16),
            pltpu.VMEM((32, 128), BF16),
            pltpu.VMEM((2, ROWS, ROWS), BF16),
            pltpu.VMEM((CHUNKS, 128, LANES), F32),
            pltpu.VMEM((8, ROWS + 120, LANES), F32),
            pltpu.VMEM((HALF_ROWS, LANES), F32),
            dma((2, CHUNKS)), dma((2,)), dma((7, UNITS)),
            dma((1,)), dma((PARTS,)), dma((2, 2)), dma((2, 2, PARTS)),
            dma((1,)), dma((4, MESSAGES)),
            dma((1,)), dma((CHUNKS, 2)), dma((1,)), dma((CHUNKS, 2)),
            dma((2,)), dma((2,)), dma((1,)), dma((1,)), dma, dma,
        ],
        compiler_params=pltpu.CompilerParams(
            collective_id=0, has_side_effects=True, vmem_limit_bytes=56 * 1024 * 1024),
        name="hyena",
    )(tokens, input_weight, filter_taps, decay_rates.reshape(1, -1), skip_gain.reshape(1, -1), owners.reshape(1, -1))
    def place(a, b, a_out, b_out):
        a_out[...] = a[...]
        b_out[...] = b[...]

    gated, handed = pl.pallas_call(
        place, out_shape=(jax.ShapeDtypeStruct((ROWS, 1024), BF16),) * 2, in_specs=[vmem, vmem], out_specs=(vmem, vmem),
        name="results",
    )(gated, handed)
    return gated, handed.reshape(32, 8, 1024)


def solution(mesh):
    return jax.shard_map(
        per_device,
        mesh=mesh,
        in_specs=(P("seq", "chan"), P(None, "seq", "chan"), P(None, "chan"), P("chan"), P("chan"), P("seq", None)),
        out_specs=(P("seq", "chan"), P("seq", None, "chan")),
        check_vma=False,
    )
```

```python
import jax
import jax.numpy as jnp
from jax import lax
from jax.experimental import pallas as pl
from jax.experimental.pallas import tpu as pltpu
from jax.sharding import PartitionSpec as P

MESH = pl.DeviceIdType.MESH
F32, BF16 = jnp.float32, jnp.bfloat16
CHUNKS, LANES = 4, 128
ROWS, HALF = 256, 512
PARTS = 4
SUB, MESSAGES = ROWS // PARTS, 4 * PARTS
ORDER = [(m + PARTS // 2) % PARTS for m in range(PARTS)]
HALF_ROWS = ROWS // 2
AHEAD, UNITS, W_AHEAD, W_LEAD = 5, 3 * CHUNKS, 3, 1


def kernel(tok, wgt, taps_in, decay, skip, owners, gated, handed,
           wbuf, wother, tbuf, txbuf, own, osend, orecv, qbuf, ubuf, hrecv, psend, pbuf, gsend, grecv,
           mine, theirs, sel, taps, shifts, prior,
           wl, ws, wr, txs, txr, tzs, tzr, tys, tyr, os_, or_, hs, hr, ps, pr, gs, gr, ms, mr):
    s, c = lax.axis_index("seq"), lax.axis_index("chan")
    core, x, zh = s % 2, (s // 2) % 4, s // 8
    zl, y = c // 4, c % 4
    zo, x2 = 1 - zh, (x + 2) % 4

    def dev(zh_, x_, core_, zl_, y_):
        return ((zh_ * 4 + x_) * 2 + core_, zl_ * 4 + y_)

    def remote(src, dst, ss, rs, to):
        return pltpu.make_async_remote_copy(
            src_ref=src, dst_ref=dst, send_sem=ss, recv_sem=rs, device_id=to, device_id_type=MESH)

    def at(start, size):
        return pl.ds(pl.multiple_of(start * size, size), size)

    def group(j):
        return ((x + j % 2) // 2) % 2

    def beside(j):
        up = 1 - 2 * ((x + j) % 2)
        return (x + 4 + up) % 4

    def across(j):
        up = 1 - 2 * ((x + j + 1) % 2)
        return (x + 4 + up) % 4

    def kb(xx):
        return xx * 2 + core

    def load(j):
        return pltpu.make_async_copy(wgt.at[:, :, at(2 * j + group(j), LANES)], wbuf.at[j, kb(x)], wl.at[0, j])

    def load_other(j):
        return pltpu.make_async_copy(wgt.at[:, :, at(2 * j + 1 - group(j), LANES)], wother.at[j], wl.at[1, j])

    @pl.loop(0, CHUNKS)
    def _(j):
        load(j).start()
        load_other(j).start()

    barrier = pltpu.get_barrier_semaphore()

    partners = [dev(zh, (x + d) % 4, core, zl, y) for d in (1, 2, 3)] + [dev(zh, x, 1 - core, zl, y)]
    partners += [dev(zo, x, core, zl, y), dev(zh, x, core, 1 - zl, y), dev(zo, x, core, 1 - zl, y)]
    partners += [dev(zh, x, core, zl, (y + d) % 4) for d in (1, 3)]
    for partner in partners:
        pl.semaphore_signal(barrier, inc=1, device_id=partner, device_id_type=MESH)
    pl.semaphore_wait(barrier, len(partners))

    def w_beside(v):
        block = wbuf.at[v // 3, kb(x), v % 3]
        return remote(block, block, ws.at[0], wr.at[0, v], dev(zh, beside(v // 3), core, zl, y))

    def w_across(v):
        return remote(wother.at[v // 3, v % 3], wbuf.at[v // 3, kb(x), v % 3], ws.at[0], wr.at[1, v],
                      dev(zh, across(v // 3), core, zl, y))

    def w_far(v):
        block = wbuf.at[v // 3, kb(across(v // 3)), v % 3]
        return remote(block, block, ws.at[0], wr.at[2, v], dev(zh, beside(v // 3), core, zl, y))

    def w_pair(j, k):
        block = wbuf.at[j, kb((x + k) % 4)]
        return remote(block, block, ws.at[1], wr.at[3 + k, j], dev(zh, x, 1 - core, zl, y))

    def w_send(v):
        @pl.when(v % 3 == 0)
        def _():
            load(v // 3).wait()
            load_other(v // 3).wait()

        w_beside(v).start()
        w_across(v).start()

    def w_step(v):
        @pl.when(v < UNITS)
        def _():
            w_across(v).wait_recv()
            w_far(v).start()
            w_beside(v).wait_recv()

            @pl.when(v + W_AHEAD < UNITS)
            def _():
                w_send(v + W_AHEAD)

        @pl.when((v >= 1) & (v <= UNITS))
        def _():
            w_far(v - 1).wait_recv()

            @pl.when(v % 3 == 0)
            def _():
                for k in range(4):
                    w_pair(v // 3 - 1, k).start()

    def t_x(sub):
        return remote(tok.at[at(sub, SUB)], txbuf.at[at(sub, SUB)], txs.at[0], txr.at[sub], dev(zh, x2, core, zl, y))

    def t_z(e, sub, d):
        src = txbuf if e else tok
        return remote(src.at[at(sub, SUB)], tbuf.at[y, zh, e, at(sub, SUB)], tzs.at[e, d], tzr.at[zh, e, sub],
                      dev(zl, x, core, d, y))

    def t_own(e, sub):
        src = txbuf if e else tok
        return pltpu.make_async_copy(src.at[at(sub, SUB)], tbuf.at[y, zh, e, at(sub, SUB)], tzr.at[zh, e, sub])

    def stays(d):
        return jnp.logical_and(zl == zh, zl == d)

    def t_along_z(e, sub):
        for d in (0, 1):
            @pl.when(stays(d))
            def _():
                t_own(e, sub).start()

            @pl.when(jnp.logical_not(stays(d)))
            def _():
                t_z(e, sub, d).start()

    early = x // 2

    def block_of(m):
        r = m // PARTS
        return jnp.where(r < 2, zo, zh), jnp.where(r < 2, r, (early + r) % 2)

    def part_of(m):
        return (m + PARTS // 2) % PARTS

    def t_piece(yy, m):
        z, e = block_of(m)
        return tbuf.at[yy, z, e, at(part_of(m), SUB)]

    def t_near(m, k):
        piece = t_piece(y, m)
        return remote(piece, piece, tys.at[0], tyr.at[k, m], dev(zh, x, core, zl, (y + 1 + 2 * k) % 4))

    def t_next(m, k):
        z, e = block_of(m)
        piece = tbuf.at[(y + 3 - 2 * k) % 4, z, e, at(part_of(m) * 2 + k, SUB // 2)]
        return remote(piece, piece, tys.at[0], tyr.at[2 + k, m], dev(zh, x, core, zl, (y + 1 + 2 * k) % 4))

    def t_along_y(m):
        z, e = block_of(m)
        piece = t_piece(y, m)
        pltpu.make_async_copy(piece, piece, tzr.at[z, e, part_of(m)]).wait()
        t_near(m, 0).start()
        t_near(m, 1).start()

    for sub in ORDER:
        t_x(sub).start()
        t_along_z(0, sub)
    for v in range(W_AHEAD):
        w_send(v)

    iota = lambda shape, axis: lax.broadcasted_iota(jnp.int32, shape, axis)
    dot = lambda a, b, dims: lax.dot_general(a, b, (dims, ((), ())), preferred_element_type=F32)
    onehot = (jnp.broadcast_to(owners[...], (32, 32)) == iota((32, 32), 0)).astype(F32)
    before = (iota((32, 32), 0) < iota((32, 32), 1)).astype(BF16)
    earlier = dot(onehot.astype(BF16), before, ((1,), (0,)))
    target = owners[...].astype(F32) * 2.0 + jnp.sum(earlier * onehot, axis=0, keepdims=True)
    place = (jnp.broadcast_to(target, (32, 32)) == iota((32, 32), 0).astype(F32)).astype(F32)
    mine[...] = jnp.concatenate([place, jnp.zeros((32, 96), F32)], axis=1).astype(BF16)

    def m_copy():
        return remote(mine, theirs, ms, mr, dev(zh, x2, core, zl, y))

    m_copy().start()
    t_along_y(0)
    t_along_y(1)
    w_step(0)
    for step, sub in enumerate(ORDER):
        t_x(sub).wait_recv()
        t_along_z(1, sub)
        if step + 2 < AHEAD:
            t_along_y(step + 2)
        if step + 1 < W_LEAD:
            w_step(step + 1)

    def order(place):
        spread = (iota((ROWS, 32), 0) // 8 == iota((ROWS, 32), 1)).astype(BF16)
        part = dot(spread, place[:, :32], ((1,), (0,))).astype(BF16)
        whole = dot(part, spread, ((1,), (1,)))
        same = (iota((ROWS, ROWS), 0) % 8 == iota((ROWS, ROWS), 1) % 8).astype(F32)
        return (whole * same).astype(BF16)

    sel[0] = order(mine[...])
    m_copy().wait_recv()
    sel[1] = order(theirs[...])

    lag = iota((128, LANES), 0)

    @pl.loop(0, CHUNKS)
    def _(j):
        cols = at(2 * j + group(j), LANES)
        value = taps_in[:, cols] * jnp.exp(-decay[:, cols] * lag.astype(F32))
        taps[j] = value + jnp.where(lag == 0, skip[:, cols], 0.0)

    def matmul(j, z, e):
        t = jnp.concatenate([tbuf[yy, z, e] for yy in range(4)], axis=1)
        w = jnp.concatenate([jnp.concatenate([wbuf[j, k, p] for k in range(8)], axis=0) for p in range(3)], axis=1)
        return jnp.dot(t, w, preferred_element_type=F32)

    def o_copy(j, e):
        return remote(osend.at[j, e], orecv.at[j, e], os_.at[0], or_.at[j, e], dev(zo, x, core, zl, y))

    def h_copy(j, e):
        xe = (x + 2 * e) % 4
        to = beside(j)
        same = jnp.where((xe + 1) % 4 == to, 0, 1)
        to_x, to_zh = jnp.where(core == 0, x, to), jnp.where(core == 0, zh, (zh + xe // 3) % 2)
        to_e = jnp.where(core == 0, e, same)
        return remote(ubuf.at[j, e, pl.ds(128, 128)], hrecv.at[j, to_e], hs.at[0], hr.at[j, to_e],
                      dev(to_zh, to_x, 1 - core, zl, y))

    def p_copy(e, o):
        to, source = (s + o) % 16, (zh * 4 + (x + 2 * e) % 4) * 2 + core
        return remote(psend.at[e, :, at(to, 16)], pbuf.at[e, :, at(source, 16)], ps.at[e], pr.at[e], (to, c))

    def stage_pages(e):
        @pl.loop(1, 16)
        def _(o):
            p_copy(e, o).start()

        source = (zh * 4 + (x + 2 * e) % 4) * 2 + core
        pbuf[e, :, at(source, 16)] = psend[e, :, at(s, 16)]

    def g_copy(j, rows):
        return remote(gsend.at[j, rows], grecv.at[j, rows], gs.at[0], gr.at[0], dev(zh, x2, core, zl, y))

    def matmul_pair(pair, z, e, rows):
        t = jnp.concatenate([tbuf[yy, z, e, rows] for yy in range(4)], axis=1)
        w = jnp.concatenate([jnp.concatenate([wbuf[2 * pair + q, k, p] for k in range(8)], axis=0)
                             for q in (0, 1) for p in range(3)], axis=1)
        both = jnp.dot(t, w, preferred_element_type=F32)
        return both[:, :3 * LANES], both[:, 3 * LANES:]

    def stage_other(n):
        e = jnp.where(n < 2, 0, jnp.where(n % 2 == 0, early, 1 - early))
        j = jnp.where(n < 2, n, n // 2 + 1)
        osend[j, e] = matmul(j, zo, e).astype(BF16)
        o_copy(j, e).start()

    def stage_other_half(half):
        rows = at(half, HALF_ROWS)
        for j, part in enumerate(matmul_pair(0, zo, 1, rows)):
            osend[j, 1, rows] = part.astype(BF16)
            remote(osend.at[j, 1, rows], orecv.at[j, 1, rows], os_.at[0], or_.at[j, 1], dev(zo, x, core, zl, y)).start()

    def stage_own(n):
        late = n // 4
        pair = jnp.where(n < 4, n // 2, n % 2)
        rows = at(jnp.where(n < 4, n % 2, 1 - (n - 4) // 2), HALF_ROWS)
        e = jnp.where(n < 4, early, 1 - early)
        for q, part in enumerate(matmul_pair(pair, zh, e, rows)):
            own[late, 2 * pair + q, rows] = part

    def stage_u(n):
        late = n // 8
        j = jnp.where(n < 8, n // 2, n % 4)
        half = 1 - jnp.where(n < 8, n % 2, (n - 8) // 4)
        e, rows = jnp.where(n < 8, early, 1 - early), at(half, HALF_ROWS)

        @pl.when(half == 1)
        def _():
            o_copy(j, e).wait_recv()

        full = (own[late, j, rows] + orecv[j, e, rows].astype(F32)).astype(BF16)
        qbuf[j, e, rows] = full[:, :LANES]
        ubuf[j, e, rows] = (full[:, LANES:2 * LANES].astype(F32) * full[:, 2 * LANES:].astype(F32)).astype(BF16)

        @pl.when(half == 1)
        def _():
            h_copy(j, e).start()

        @pl.when((n == 7) | (n == 15))
        def _():
            @pl.loop(0, CHUNKS)
            def _(jj):
                psend[e, jj] = jnp.dot(sel[e], ubuf[jj, e], preferred_element_type=F32).astype(BF16)

            stage_pages(e)

    def wait_prior(j, e):
        pltpu.make_async_copy(hrecv.at[j, e], hrecv.at[j, e], hr.at[j, e]).wait()
        first = (zh == 0) & (core == 0) & ((x + 2 * e) % 4 == 0)
        return jnp.where(first, 0.0, hrecv[j, e].astype(F32))

    def filtered(j, before, u):
        count = u.shape[0] // 16
        ext = jnp.concatenate([before, u.astype(F32)], axis=0)
        for b in range(8):
            shifts[b, :ext.shape[0] - 8] = ext[8 - b:ext.shape[0] - b]

        def stream(groups, tap, data):
            sums = [jnp.zeros((8, LANES), F32) for _ in range(groups)]
            for b in range(8):
                x_ = [data(b, m) for m in range(groups + 7)]
                for a in range(8):
                    weight = jnp.broadcast_to(tap(b, a), (8, LANES))
                    for r in range(groups):
                        sums[r] = sums[r] + weight * x_[r - a + 7]
            return sums

        def rows_of(b, m):
            return shifts[b, 8 * m:8 * m + 8]

        def tap_of(b, a):
            return taps[j, 8 * a + b:8 * a + b + 1]

        even = stream(count, lambda b, a: tap_of(b, 2 * a), lambda b, m: rows_of(b, 2 * m + 1))
        odd = stream(count + 1, lambda b, a: tap_of(b, 2 * a + 1), lambda b, m: rows_of(b, 2 * m))
        both = stream(count, lambda b, a: tap_of(b, 2 * a) + tap_of(b, 2 * a + 1),
                      lambda b, m: rows_of(b, 2 * m + 1) + rows_of(b, 2 * m + 2))
        return jnp.concatenate(
            [piece for r in range(count) for piece in (even[r] + odd[r], both[r] - even[r] - odd[r + 1])], axis=0)

    def finish(j, e, rows, z):
        out = (qbuf[j, e, rows].astype(F32) * z).astype(BF16)

        @pl.when(e == 1)
        def _():
            gsend[j, rows] = out
            g_copy(j, rows).start()

        @pl.when(e == 0)
        def _():
            gated[rows, at(2 * j + group(j), LANES)] = out

    def stage_filter(j, half):
        @pl.when(half == 0)
        def _():
            prior[...] = wait_prior(j, early)

        @pl.when(half == 1)
        def _():
            prior[...] = ubuf[j, early, :HALF_ROWS].astype(F32)

        rows = at(half, HALF_ROWS)
        finish(j, early, rows, filtered(j, prior[...], ubuf[j, early, rows]))

    def stage_filter_whole(j):
        e = 1 - early
        finish(j, e, pl.ds(0, ROWS), filtered(j, wait_prior(j, e), ubuf[j, e]))

    def others_done(i):
        return jnp.where(i < 4, 0, jnp.where(i < 9, jnp.minimum(i // 2 - 1, 2), jnp.where(i < 12, 4, 6)))

    def owns_done(i):
        return jnp.where(i < 13, 0, jnp.where(i < 16, 2 * (i - 12), 6))

    def us_done(i):
        return jnp.where(i < 13, 0, jnp.where(i == 13, 4, jnp.where(i == 14, 6, jnp.where(i == 15, 12, 16))))

    def filters_done(i):
        return jnp.where(i < 13, 0, jnp.where(i == 13, 1, jnp.where(i == 14, 3, jnp.where(i == 15, 4, 12))))

    @pl.loop(0, MESSAGES + 1)
    def _(i):
        @pl.when(i < MESSAGES)
        def _():
            t_near(i, 0).wait_recv()
            t_next(i, 0).start()
            t_near(i, 1).wait_recv()
            t_next(i, 1).start()

        @pl.when(i + AHEAD < MESSAGES)
        def _():
            t_along_y(i + AHEAD)

        w_step(i + W_LEAD)

        done = i + W_LEAD - 4

        @pl.when((done >= 0) & (done <= 9) & (done % 3 == 0))
        def _():
            for k in range(4):
                w_pair(done // 3, k).wait_recv()

        @pl.when(i >= 1)
        def _():
            t_next(i - 1, 0).wait_recv()
            t_next(i - 1, 1).wait_recv()

        @pl.loop(others_done(i - 1), others_done(i))
        def _(n):
            stage_other(n)

        @pl.when((i == 6) | (i == 8))
        def _():
            stage_other_half((8 - i) // 2)

        @pl.loop(owns_done(i - 1), owns_done(i))
        def _(n):
            stage_own(n)

        @pl.loop(us_done(i - 1), us_done(i))
        def _(n):
            @pl.when((n == 12) | (n == 14))
            def _():
                stage_own(n // 2)

            stage_u(n)

        @pl.loop(filters_done(i - 1), filters_done(i))
        def _(n):
            sooner = (n < 4) | ((n // 4 + early) % 2 == 0)

            @pl.when(sooner)
            def _():
                stage_filter(n % 4, jnp.where(n < 4, 1, 0))

            @pl.when(jnp.logical_not(sooner))
            def _():
                stage_filter_whole(n % 4)

    def sent(ref, sem):
        pltpu.make_async_copy(ref, ref, sem).wait()

    sent(tbuf.at[pl.ds(0, 3)], tys.at[0])
    sent(wbuf.at[pl.ds(0, 2), pl.ds(0, 6)], ws.at[0])
    sent(wbuf.at[pl.ds(0, 2)], ws.at[1])
    sent(osend, os_.at[0])
    sent(hrecv, hs.at[0])
    sent(mine, ms)
    sent(txbuf, txs.at[0])
    for e in (0, 1):
        for d in (0, 1):
            @pl.when(jnp.logical_not(stays(d)))
            def _():
                sent(txbuf, tzs.at[e, d])

    for e in (0, 1):
        sent(pbuf.at[e, :, pl.ds(0, 240)], ps.at[e])
        sent(pbuf.at[e, :, pl.ds(0, 240)], pr.at[e])

    @pl.loop(0, 16)
    def _(source):
        rows = at(source, 16)
        for e in (0, 1):
            there = (source // 2 + 2 * e) % 4
            for j in range(CHUNKS):
                handed[rows, at(2 * j + ((there + j % 2) // 2) % 2, LANES)] = pbuf[e, j, rows]

    sent(gsend, gr.at[0])
    for j in range(CHUNKS):
        gated[:, at(2 * j + 1 - group(j), LANES)] = grecv[j]
    sent(gsend, gs.at[0])


def per_device(tokens, input_weight, filter_taps, decay_rates, skip_gain, owners):
    dma = pltpu.SemaphoreType.DMA
    vmem, any_ = pl.BlockSpec(memory_space=pltpu.VMEM), pl.BlockSpec(memory_space=pl.ANY)
    gated, handed = pl.pallas_call(
        kernel,
        out_shape=(jax.ShapeDtypeStruct((ROWS, 1024), BF16), jax.ShapeDtypeStruct((ROWS, 1024), BF16)),
        in_specs=[any_, any_, vmem, vmem, vmem, vmem],
        out_specs=(vmem, vmem),
        scratch_shapes=[
            pltpu.VMEM((CHUNKS, 8, 3, HALF, LANES), BF16),
            pltpu.VMEM((CHUNKS, 3, HALF, LANES), BF16),
            pltpu.VMEM((4, 2, 2, ROWS, 1024), BF16),
            pltpu.VMEM((ROWS, 1024), BF16),
            pltpu.VMEM((2, CHUNKS, ROWS, 3 * LANES), F32),
            pltpu.VMEM((CHUNKS, 2, ROWS, 3 * LANES), BF16),
            pltpu.VMEM((CHUNKS, 2, ROWS, 3 * LANES), BF16),
            pltpu.VMEM((CHUNKS, 2, ROWS, LANES), BF16),
            pltpu.VMEM((CHUNKS, 2, ROWS, LANES), BF16),
            pltpu.VMEM((CHUNKS, 2, 128, LANES), BF16),
            pltpu.VMEM((2, CHUNKS, ROWS, LANES), BF16),
            pltpu.VMEM((2, CHUNKS, ROWS, LANES), BF16),
            pltpu.VMEM((CHUNKS, ROWS, LANES), BF16),
            pltpu.VMEM((CHUNKS, ROWS, LANES), BF16),
            pltpu.VMEM((32, 128), BF16),
            pltpu.VMEM((32, 128), BF16),
            pltpu.VMEM((2, ROWS, ROWS), BF16),
            pltpu.VMEM((CHUNKS, 128, LANES), F32),
            pltpu.VMEM((8, ROWS + 120, LANES), F32),
            pltpu.VMEM((HALF_ROWS, LANES), F32),
            dma((2, CHUNKS)), dma((2,)), dma((7, UNITS)),
            dma((1,)), dma((PARTS,)), dma((2, 2)), dma((2, 2, PARTS)),
            dma((1,)), dma((4, MESSAGES)),
            dma((1,)), dma((CHUNKS, 2)), dma((1,)), dma((CHUNKS, 2)),
            dma((2,)), dma((2,)), dma((1,)), dma((1,)), dma, dma,
        ],
        compiler_params=pltpu.CompilerParams(
            collective_id=0, has_side_effects=True, vmem_limit_bytes=56 * 1024 * 1024),
        name="hyena",
    )(tokens, input_weight, filter_taps, decay_rates.reshape(1, -1), skip_gain.reshape(1, -1), owners.reshape(1, -1))
    def place(a, b, a_out, b_out):
        a_out[...] = a[...]
        b_out[...] = b[...]

    gated, handed = pl.pallas_call(
        place, out_shape=(jax.ShapeDtypeStruct((ROWS, 1024), BF16),) * 2, in_specs=[vmem, vmem], out_specs=(vmem, vmem),
        name="results",
    )(gated, handed)
    return gated, handed.reshape(32, 8, 1024)


def solution(mesh):
    return jax.shard_map(
        per_device,
        mesh=mesh,
        in_specs=(P("seq", "chan"), P(None, "seq", "chan"), P(None, "chan"), P("chan"), P("chan"), P("seq", None)),
        out_specs=(P("seq", "chan"), P("seq", None, "chan")),
        check_vma=False,
    )
```
